32 devices in a mesh: row: 8 (over z, y), col: 4 (over x, core).
Axes of the slice: x: 2, y: 2, z: 4, core: 2. Of those that a mesh axis runs over, the one named last changes fastest.
Arguments:
- tensor: bfloat16 [4, 4096, 8192], P(None, 'row', 'col'), may hold values from -6 to 6
- second_factor: float32 [8192, 128], P(('col', 'row')), as said below
- time_factor: float32 [4, 128], replicated, may hold values from 0.5 to 1.5
Outputs:
- first_factor: float32 [4096, 128], P(('row', 'col'))
- column_scales: float32 [128], replicated
The draws below stay inside these ranges and needn't reach their ends.
Inputs may be any that keep to these rules, and one draw needn't show every extreme that they name: `second_factor`: real numbers of magnitude at most 120 / sqrt(8192).
All inputs are finite; a program needn't handle non-finite values.
Results may differ from the reference program's by a relative error of at most 0.0056.
Values may be sent and summed in bfloat16 or wider, within the bound.
No kernel may reach another device: no remote copies, remote signals or barrier semaphores. Data moves between devices by JAX's collectives and lax.ppermute only.
A program may use at most 64 MiB of HBM per device.

```python
import math
import jax
import jax.numpy as jnp
from jax import lax

R = 128
K = 4
IR = 512
I = 4096
J = 8192


def correlated(noise, columns, limit):
    total = jnp.zeros((noise.shape[0], columns), jnp.float32)
    weight_sum = 0.0
    for lag in range(16):
        weight = 0.7 ** lag
        total = total + weight * noise[:, 15 - lag:15 - lag + columns]
        weight_sum = weight_sum + weight * weight
    return jnp.clip(total / math.sqrt(weight_sum), -limit, limit)


def draw_second_factor(key, part):
    key = jax.random.fold_in(key, 7)
    base_key, col_key = jax.random.split(key)
    noise = jnp.clip(jax.random.normal(base_key, (J, R + 15), jnp.float32), -4.0, 4.0)
    base = correlated(noise, R, 4.0)
    spread = jnp.exp(jax.random.uniform(col_key, (R,), jnp.float32, 0.0, math.log(10.0)))
    rising = jnp.power(3.0, jnp.arange(J, dtype=jnp.float32) / J)
    return (base * rising[:, None] * spread[None, :] / math.sqrt(J)).astype(jnp.float32)


def steps_of(own_key, shape, cuts, least, high):
    level, own = 1.0, jax.random.fold_in(own_key, 6)
    for axis_at, parts in cuts:
        heights = jnp.exp(jax.random.uniform(jax.random.fold_in(own, axis_at), (parts,), jnp.float32, least / len(cuts), high / len(cuts)))
        level = level * jnp.repeat(heights, shape[axis_at] // parts).reshape([-1 if axis == axis_at else 1 for axis in range(len(shape))])
    return level


def normal_values(stream_key, shape, deviation, reach, pieces=(), kind=jnp.bfloat16):
    result = jax.random.normal(stream_key, shape, jnp.float32) * deviation
    if len(pieces) > 0:
        result = steps_of(stream_key, shape, pieces, -0.22, 0.18) * result
    return jnp.clip(result, min=-reach, max=reach).astype(kind)


def setup_inputs(seed: int = 0) -> dict:
    key_of = jax.random.split(jax.random.key(seed), 4)
    tensor = normal_values(key_of[0], (K, I, J), 1.0, 6.0, ((1, 8), (2, 4)))
    second_factor = draw_second_factor(jax.random.fold_in(key_of[3], 71), 0)
    time_factor = jnp.clip(jax.random.uniform(key_of[2], (K, R), jnp.float32, 0.5, 1.5), 0.5, 1.5)
    return dict(tensor=tensor, second_factor=second_factor, time_factor=time_factor)


def reference(tensor, second_factor, time_factor):
    low = second_factor.astype(jnp.bfloat16)
    count = I // IR

    def row_block(index):
        part = lax.dynamic_slice_in_dim(tensor, index * IR, IR, 1)
        total = jnp.zeros((IR, R), jnp.float32)
        for snap in range(K):
            total = total + time_factor[snap][None, :] * jnp.dot(part[snap].astype(jnp.float32), low.astype(jnp.float32), preferred_element_type=jnp.float32)
        return total
    mttkrp = lax.map(row_block, jnp.arange(count, dtype=jnp.int32)).reshape(I, R)
    gram = jnp.dot(second_factor.T.astype(jnp.float32), second_factor.astype(jnp.float32), precision=lax.Precision.HIGHEST, preferred_element_type=jnp.float32)
    time_gram = jnp.dot(time_factor.T.astype(jnp.float32), time_factor.astype(jnp.float32), precision=lax.Precision.HIGHEST, preferred_element_type=jnp.float32)
    system = gram * time_gram
    lower = jnp.linalg.cholesky(system)
    solved = jax.scipy.linalg.cho_solve((lower, True), mttkrp.T).T
    squares = lax.optimization_barrier(jnp.sum(solved * solved, axis=0))
    column_scales = jnp.sqrt(squares / I + 1e-06)
    return (solved / column_scales[None, :], column_scales)
```

```python
import functools

import jax
import jax.numpy as jnp
from jax import lax
from jax.experimental import pallas as pl
from jax.experimental.pallas import tpu as pltpu
from jax.sharding import PartitionSpec as P

F32, BF16 = jnp.float32, jnp.bfloat16
VMEM = pl.BlockSpec(memory_space=pltpu.VMEM)
BLOCK = 16


def tdot(a, b):
    return lax.dot_general(a, b, (((0,), (0,)), ((), ())), preferred_element_type=F32)


def split3(x):
    hi = x.astype(BF16)
    rest = x - hi.astype(F32)
    mid = rest.astype(BF16)
    return hi, mid, (rest - mid.astype(F32)).astype(BF16)


def prepare_kernel(factor_ref, out_ref):
    rows, rank = factor_ref.shape
    factor = factor_ref[...]
    low = factor.astype(BF16)
    residual = (factor - low.astype(F32)).astype(BF16)
    cross = tdot(low, residual)
    rest = cross + cross.T + tdot(residual, residual)
    out_ref[:rows, :] = low
    out_ref[rows:, :] = rest.astype(BF16)


def mttkrp_kernel(owners, tensor_ref, time_ref, *refs):
    parts, (keep_ref, send_ref, low_ref) = refs[: len(owners)], refs[len(owners) :]
    snaps, own_rows, own_cols = tensor_ref.shape
    rank = time_ref.shape[1]
    depth = parts[0].shape[0] - rank
    row, col = lax.axis_index("row"), lax.axis_index("col")
    cols = lax.axis_size("col")
    piece = own_rows // cols
    gram = jnp.zeros((rank, rank), F32)
    for owner, part in zip(owners, parts):
        start = pl.multiple_of(lax.bitwise_xor(row, owner) * depth, depth)
        low_ref[pl.ds(start, depth), :] = part[:depth, :]
        gram = gram + part[depth:, :].astype(F32)
    low = low_ref[...]
    gram = gram + tdot(low, low)
    total = [
        jnp.dot(tensor_ref[snap], low, preferred_element_type=F32) for snap in range(snaps)
    ]
    result = sum(total[snap] * time_ref[snap : snap + 1, :] for snap in range(snaps))
    core = lax.rem(col, 2)
    for pair in range(cols // 2):
        even = result[(2 * pair) * piece : (2 * pair + 1) * piece, :]
        odd = result[(2 * pair + 1) * piece : (2 * pair + 2) * piece, :]
        keep_ref[pair * piece : (pair + 1) * piece, :] = jnp.where(core == 0, even, odd)
        send_ref[pair * piece : (pair + 1) * piece, :] = jnp.where(core == 0, odd, even)
    send_ref[(cols // 2) * piece :, :] = gram


def negative_inverse(matrix):
    size = matrix.shape[0]
    lane = lax.broadcasted_iota(jnp.int32, (BLOCK, size), 1)
    sub = lax.broadcasted_iota(jnp.int32, (BLOCK, size), 0)
    at_row = lax.broadcasted_iota(jnp.int32, (size, size), 0)
    at_col = lax.broadcasted_iota(jnp.int32, (size, size), 1)
    for begin in range(0, size, BLOCK):
        end = begin + BLOCK
        panel = matrix[begin:end, :]
        diag = [
            jnp.broadcast_to(panel[:, begin + j : begin + j + 1], (BLOCK, size))
            for j in range(BLOCK)
        ]
        inside = (lane >= begin) & (lane < end)
        work = jnp.where(inside, jnp.where(lane - begin == sub, -1.0, 0.0), panel)
        solved = jnp.zeros((BLOCK, size), F32)
        for k in range(BLOCK):
            scale = lax.rsqrt(jnp.broadcast_to(diag[k][k : k + 1, :], (BLOCK, size)))
            lower = jnp.where(sub > k, diag[k] * scale, 0.0)
            pivot = jnp.broadcast_to(work[k : k + 1, :], (BLOCK, size)) * scale
            solved = jnp.where(sub == k, pivot, solved)
            work = work - lower * pivot
            for j in range(k + 1, BLOCK):
                diag[j] = diag[j] - lower * (
                    jnp.broadcast_to(diag[j][k : k + 1, :], (BLOCK, size)) * scale
                )
        hi, mid, lo = split3(solved)
        update = tdot(
            jnp.concatenate([hi, hi, mid, mid, hi, lo], 0),
            jnp.concatenate([hi, mid, hi, mid, lo, hi], 0),
        )
        swept = (at_row >= begin) & (at_row < end) | (at_col >= begin) & (at_col < end)
        matrix = jnp.where(swept, 0.0, matrix) - update
    return matrix


def solve_kernel(own_ref, got_ref, time_ref, solved_ref, squares_ref):
    piece = solved_ref.shape[0]
    time = time_ref[...]
    time_gram = lax.dot_general(
        time,
        time,
        (((0,), (0,)), ((), ())),
        precision=lax.Precision.HIGHEST,
        preferred_element_type=F32,
    )
    total = own_ref[...] + sum(got_ref[at] for at in range(got_ref.shape[0]))
    inverse = negative_inverse(total[piece:, :] * time_gram)
    solved = -jnp.dot(
        total[:piece, :],
        inverse,
        precision=lax.Precision.HIGHEST,
        preferred_element_type=F32,
    )
    solved_ref[...] = solved
    squares = jnp.sum(solved * solved, axis=0, keepdims=True)
    squares_ref[...] = jnp.broadcast_to(squares, squares_ref.shape)


def normalize_kernel(total_rows, solved_ref, squares_ref, out_ref, scales_ref):
    mean = jnp.sum(squares_ref[...], axis=0, keepdims=True) / total_rows
    scales = jnp.sqrt(mean + 1e-06)
    scales_ref[...] = scales
    out_ref[...] = solved_ref[...] / scales


def shifted(value, axis, offset, groups):
    return lax.ppermute(value, axis, [(at, at ^ offset) for at in range(groups)])


def per_device(tensor, second_factor, time_factor):
    snaps, own_rows, own_cols = tensor.shape
    depth, rank = second_factor.shape
    rows, cols = lax.axis_size("row"), lax.axis_size("col")
    piece = own_rows // cols
    pairs = cols // 2

    message = pl.pallas_call(
        prepare_kernel,
        out_shape=jax.ShapeDtypeStruct((depth + rank, rank), BF16),
        in_specs=[VMEM],
        out_specs=VMEM,
    )(second_factor)
    owners = tuple(range(rows))
    messages = [message] + [shifted(message, "row", at, rows) for at in owners[1:]]
    keep, send = pl.pallas_call(
        functools.partial(mttkrp_kernel, owners),
        out_shape=(
            jax.ShapeDtypeStruct((pairs * piece, rank), F32),
            jax.ShapeDtypeStruct((pairs * piece + rank, rank), F32),
        ),
        in_specs=[VMEM] * (2 + rows),
        out_specs=(VMEM, VMEM),
        scratch_shapes=[pltpu.VMEM((rows * depth, rank), BF16)],
        compiler_params=pltpu.CompilerParams(vmem_limit_bytes=32 * 2**20),
    )(tensor, time_factor, *messages)

    got = shifted(send, "col", 1, cols)
    part = pairs * piece
    sums = keep + got[:part]
    gram = send[part:] + got[part:]
    place = lax.axis_index("col") // 2
    own = jnp.concatenate([lax.dynamic_slice_in_dim(sums, place * piece, piece, 0), gram], 0)
    others = []
    for offset in range(1, pairs):
        there = lax.bitwise_xor(place, offset)
        out = jnp.concatenate([lax.dynamic_slice_in_dim(sums, there * piece, piece, 0), gram], 0)
        others.append(shifted(out, "col", 2 * offset, cols))
    solved, squares = pl.pallas_call(
        solve_kernel,
        out_shape=(
            jax.ShapeDtypeStruct((piece, rank), F32),
            jax.ShapeDtypeStruct((rows * cols, rank), F32),
        ),
        in_specs=[VMEM] * 3,
        out_specs=(VMEM, VMEM),
    )(own, jnp.stack(others), time_factor)
    squares = lax.all_to_all(squares, ("row", "col"), 0, 0, tiled=True)
    first_factor, scales = pl.pallas_call(
        functools.partial(normalize_kernel, own_rows * rows),
        out_shape=(
            jax.ShapeDtypeStruct((piece, rank), F32),
            jax.ShapeDtypeStruct((1, rank), F32),
        ),
        in_specs=[VMEM] * 2,
        out_specs=(VMEM, VMEM),
    )(solved, squares)
    return first_factor, scales.reshape(rank)


def solution(mesh):
    in_specs = (P(None, "row", "col"), P(("col", "row"), None), P())
    out_specs = (P(("row", "col"), None), P())
    return jax.shard_map(
        per_device, mesh=mesh, in_specs=in_specs, out_specs=out_specs, check_vma=False
    )
```

```python
import functools

import jax
import jax.numpy as jnp
from jax import lax
from jax.experimental import pallas as pl
from jax.experimental.pallas import tpu as pltpu
from jax.sharding import PartitionSpec as P

F32, BF16 = jnp.float32, jnp.bfloat16
HBM = pl.BlockSpec(memory_space=pltpu.HBM)
VMEM = pl.BlockSpec(memory_space=pltpu.VMEM)
BLOCK = 16


def tdot(a, b):
    return lax.dot_general(a, b, (((0,), (0,)), ((), ())), preferred_element_type=F32)


def split3(x):
    hi = x.astype(BF16)
    rest = x - hi.astype(F32)
    mid = rest.astype(BF16)
    return hi, mid, (rest - mid.astype(F32)).astype(BF16)


def prepare_kernel(factor_ref, out_ref):
    rows, rank = factor_ref.shape
    factor = factor_ref[...]
    low = factor.astype(BF16)
    residual = (factor - low.astype(F32)).astype(BF16)
    cross = tdot(low, residual)
    rest = cross + cross.T + tdot(residual, residual)
    out_ref[:rows, :] = low
    out_ref[rows:, :] = rest.astype(BF16)


def load_kernel(owners, depth, tensor_ref, time_ref, gate_ref, slots_ref, time_out_ref, gram_ref, sems):
    del gate_ref
    row = lax.axis_index("row")
    copies = [pltpu.make_async_copy(time_ref, time_out_ref, sems.at[len(owners)])]
    for at, owner in enumerate(owners):
        start = pl.multiple_of(lax.bitwise_xor(row, owner) * depth, depth)
        copies.append(
            pltpu.make_async_copy(
                tensor_ref.at[:, :, pl.ds(start, depth)], slots_ref.at[at], sems.at[at]
            )
        )
    for copy in copies:
        copy.start()
    copies[0].wait()
    time = time_out_ref[...]
    gram_ref[...] = lax.dot_general(
        time,
        time,
        (((0,), (0,)), ((), ())),
        precision=lax.Precision.HIGHEST,
        preferred_element_type=F32,
    )
    for copy in copies[1:]:
        copy.wait()


def multiply(slots, slots_ref, time_ref, parts):
    snaps, own_rows, depth = slots_ref.shape[1:]
    rank = time_ref.shape[1]
    gram = jnp.zeros((rank, rank), F32)
    total = [jnp.zeros((own_rows, rank), F32) for _ in range(snaps)]
    for at, part in zip(slots, parts):
        low = part[:depth, :]
        gram = gram + tdot(low, low) + part[depth:, :].astype(F32)
        for snap in range(snaps):
            total[snap] = total[snap] + jnp.dot(
                slots_ref[at, snap], low, preferred_element_type=F32
            )
    return sum(total[snap] * time_ref[snap : snap + 1, :] for snap in range(snaps)), gram


def first_kernel(slots, slots_ref, time_ref, *refs):
    parts, (result_ref, gram_ref) = refs[:-2], refs[-2:]
    result_ref[...], gram_ref[...] = multiply(slots, slots_ref, time_ref, parts)


def last_kernel(slots, slots_ref, time_ref, result_ref, gram_ref, *refs):
    parts, (keep_ref, send_ref) = refs[:-2], refs[-2:]
    col, cols = lax.axis_index("col"), lax.axis_size("col")
    result, gram = result_ref[...], gram_ref[...]
    if parts:
        more, more_gram = multiply(slots, slots_ref, time_ref, parts)
        result, gram = result + more, gram + more_gram
    piece = result.shape[0] // cols
    core = lax.rem(col, 2)
    for pair in range(cols // 2):
        even = result[(2 * pair) * piece : (2 * pair + 1) * piece, :]
        odd = result[(2 * pair + 1) * piece : (2 * pair + 2) * piece, :]
        keep_ref[pair * piece : (pair + 1) * piece, :] = jnp.where(core == 0, even, odd)
        send_ref[pair * piece : (pair + 1) * piece, :] = jnp.where(core == 0, odd, even)
    send_ref[(cols // 2) * piece :, :] = gram


def chip_kernel(piece, keep_ref, sent_ref, got_ref, own_ref, *out_refs):
    place = lax.div(lax.axis_index("col"), 2)
    held = keep_ref.shape[0]
    gram = sent_ref[held:, :] + got_ref[held:, :]
    for offset, out_ref in enumerate((own_ref,) + out_refs):
        start = pl.multiple_of(lax.bitwise_xor(place, offset) * piece, piece)
        out_ref[:piece, :] = keep_ref[pl.ds(start, piece), :] + got_ref[pl.ds(start, piece), :]
        out_ref[piece:, :] = gram


def negative_inverse(matrix):
    size = matrix.shape[0]
    lane = lax.broadcasted_iota(jnp.int32, (BLOCK, size), 1)
    sub = lax.broadcasted_iota(jnp.int32, (BLOCK, size), 0)
    at_row = lax.broadcasted_iota(jnp.int32, (size, size), 0)
    at_col = lax.broadcasted_iota(jnp.int32, (size, size), 1)
    for begin in range(0, size, BLOCK):
        end = begin + BLOCK
        panel = matrix[begin:end, :]
        diag = [
            jnp.broadcast_to(panel[:, begin + j : begin + j + 1], (BLOCK, size))
            for j in range(BLOCK)
        ]
        inside = (lane >= begin) & (lane < end)
        work = jnp.where(inside, jnp.where(lane - begin == sub, -1.0, 0.0), panel)
        solved = jnp.zeros((BLOCK, size), F32)
        for k in range(BLOCK):
            scale = lax.rsqrt(jnp.broadcast_to(diag[k][k : k + 1, :], (BLOCK, size)))
            lower = jnp.where(sub > k, diag[k] * scale, 0.0)
            pivot = jnp.broadcast_to(work[k : k + 1, :], (BLOCK, size)) * scale
            solved = jnp.where(sub == k, pivot, solved)
            work = work - lower * pivot
            for j in range(k + 1, BLOCK):
                diag[j] = diag[j] - lower * (
                    jnp.broadcast_to(diag[j][k : k + 1, :], (BLOCK, size)) * scale
                )
        hi, mid, lo = split3(solved)
        update = tdot(
            jnp.concatenate([hi, hi, mid, mid, hi, lo], 0),
            jnp.concatenate([hi, mid, hi, mid, lo, hi], 0),
        )
        swept = (at_row >= begin) & (at_row < end) | (at_col >= begin) & (at_col < end)
        matrix = jnp.where(swept, 0.0, matrix) - update
    return matrix


def solve_kernel(time_gram_ref, own_ref, *refs):
    others, (solved_ref, squares_ref) = refs[:-2], refs[-2:]
    piece = solved_ref.shape[0]
    total = own_ref[...] + sum(other[...] for other in others)
    inverse = negative_inverse(total[piece:, :] * time_gram_ref[...])
    solved = -jnp.dot(
        total[:piece, :],
        inverse,
        precision=lax.Precision.HIGHEST,
        preferred_element_type=F32,
    )
    solved_ref[...] = solved
    squares = jnp.sum(solved * solved, axis=0, keepdims=True)
    squares_ref[...] = jnp.broadcast_to(squares, squares_ref.shape)


def shifted(value, axis, offset, groups):
    return lax.ppermute(value, axis, [(at, at ^ offset) for at in range(groups)])


def call(kernel, operands, in_specs, outs, scratch=()):
    return pl.pallas_call(
        kernel,
        out_shape=tuple(jax.ShapeDtypeStruct(shape, dtype) for shape, dtype in outs),
        in_specs=in_specs,
        out_specs=(VMEM,) * len(outs),
        scratch_shapes=scratch,
        compiler_params=pltpu.CompilerParams(vmem_limit_bytes=40 * 2**20),
    )(*operands)


def per_device(tensor, second_factor, time_factor):
    snaps, own_rows, own_cols = tensor.shape
    depth, rank = second_factor.shape
    rows, cols = lax.axis_size("row"), lax.axis_size("col")
    piece = own_rows // cols
    pairs = cols // 2

    (message,) = call(prepare_kernel, (second_factor,), [VMEM], [((depth + rank, rank), BF16)])
    arrived = {0: message}
    forwarded = [at for at in range(rows) if at % 2 == 1 and 2 * (at - 1) >= rows and at > 1]
    for at in range(1, rows):
        if at not in forwarded:
            arrived[at] = shifted(message, "row", at, rows)
    for at in forwarded:
        arrived[at] = shifted(arrived[at - 1], "row", 1, rows)

    early = [at for at in range(rows) if at not in forwarded]
    if depth % 128 == 0:
        owners, width = early + forwarded, depth
        first, last = [arrived[at] for at in early], [arrived[at] for at in forwarded]
    else:
        owners, width = [0], own_cols
        row = lax.axis_index("row")
        by_row = jnp.stack([arrived[at] for at in range(rows)])
        by_row = by_row[jnp.arange(rows) ^ row]
        rest = jnp.sum(by_row[:, depth:, :].astype(F32), axis=0).astype(BF16)
        low = by_row[:, :depth, :].reshape(rows * depth, rank)
        first, last = [jnp.concatenate([low, rest], 0)], []
    slots, time, time_gram = call(
        functools.partial(load_kernel, owners, width),
        (tensor, time_factor, arrived[rows // 2]),
        [HBM, HBM, VMEM],
        [((len(owners), snaps, own_rows, width), BF16), ((snaps, rank), F32), ((rank, rank), F32)],
        [pltpu.SemaphoreType.DMA((len(owners) + 1,))],
    )
    result, gram = call(
        functools.partial(first_kernel, range(len(first))),
        (slots, time, *first),
        [VMEM] * (2 + len(first)),
        [((own_rows, rank), F32), ((rank, rank), F32)],
    )
    keep, send = call(
        functools.partial(last_kernel, range(len(first), len(owners))),
        (slots, time, result, gram, *last),
        [VMEM] * (4 + len(last)),
        [((pairs * piece, rank), F32), ((pairs * piece + rank, rank), F32)],
    )

    own, *outs = call(
        functools.partial(chip_kernel, piece),
        (keep, send, shifted(send, "col", 1, cols)),
        [VMEM] * 3,
        [((piece + rank, rank), F32)] * pairs,
    )
    others = [shifted(out, "col", 2 * (at + 1), cols) for at, out in enumerate(outs)]
    solved, squares = call(
        solve_kernel,
        (time_gram, own, *others),
        [VMEM] * (1 + pairs),
        [((piece, rank), F32), ((rows * cols, rank), F32)],
    )
    squares = lax.all_to_all(squares, ("row", "col"), 0, 0, tiled=True)
    scales = jnp.sqrt(jnp.sum(squares, axis=0) / (own_rows * rows) + 1e-06)
    return solved / scales[None, :], scales


def solution(mesh):
    in_specs = (P(None, "row", "col"), P(("col", "row"), None), P())
    out_specs = (P(("row", "col"), None), P())
    return jax.shard_map(
        per_device, mesh=mesh, in_specs=in_specs, out_specs=out_specs, check_vma=False
    )
```

```python
import functools

import jax
import jax.numpy as jnp
from jax import lax
from jax.experimental import pallas as pl
from jax.experimental.pallas import tpu as pltpu
from jax.sharding import PartitionSpec as P

F32, BF16 = jnp.float32, jnp.bfloat16
HBM = pl.BlockSpec(memory_space=pltpu.HBM)
VMEM = pl.BlockSpec(memory_space=pltpu.VMEM)
TILE, STRIP, BLOCK = 8, 16, 32


def tdot(a, b):
    return lax.dot_general(a, b, (((0,), (0,)), ((), ())), preferred_element_type=F32)


def split3(x):
    hi = x.astype(BF16)
    rest = x - hi.astype(F32)
    mid = rest.astype(BF16)
    return hi, mid, (rest - mid.astype(F32)).astype(BF16)


def prepare_kernel(factor_ref, out_ref, own_ref):
    rows, rank = factor_ref.shape
    factor = factor_ref[...]
    low = factor.astype(BF16)
    residual = (factor - low.astype(F32)).astype(BF16)
    cross = tdot(low, residual)
    rest = cross + cross.T + tdot(residual, residual)
    for ref in (out_ref, own_ref):
        ref[:rows, :] = low
        ref[rows:, :] = rest.astype(BF16)


def load_kernel(owners, depth, tensor_ref, time_ref, slots_ref, time_out_ref, gram_ref, sems):
    row = lax.axis_index("row")
    copies = [pltpu.make_async_copy(time_ref, time_out_ref, sems.at[len(owners)])]
    for at, owner in enumerate(owners):
        start = pl.multiple_of(lax.bitwise_xor(row, owner) * depth, depth)
        copies.append(
            pltpu.make_async_copy(
                tensor_ref.at[:, :, pl.ds(start, depth)], slots_ref.at[at], sems.at[at]
            )
        )
    for copy in copies:
        copy.start()
    copies[0].wait()
    time = time_out_ref[...]
    gram_ref[...] = lax.dot_general(
        time,
        time,
        (((0,), (0,)), ((), ())),
        precision=lax.Precision.HIGHEST,
        preferred_element_type=F32,
    )
    for copy in copies[1:]:
        copy.wait()


def relay_kernel(loaded_ref, *refs):
    del loaded_ref
    parts, out_ref = refs[:-1], refs[-1]
    depth = parts[0].shape[0] - parts[0].shape[1]
    out_ref[:depth, :] = parts[0][:depth, :]
    if len(parts) > 1:
        rest = sum(part[depth:, :].astype(F32) for part in parts)
        out_ref[depth:, :] = rest.astype(BF16)


def gram_of(parts, depth):
    gram = 0.0
    for part in parts:
        low = part[:depth, :]
        gram = gram + tdot(low, low)
        if part.shape[0] > depth:
            gram = gram + part[depth:, :].astype(F32)
    return gram


def multiply(slots, slots_ref, time_ref, parts):
    snaps, own_rows, depth = slots_ref.shape[1:]
    rank = time_ref.shape[1]
    total = [jnp.zeros((own_rows, rank), F32) for _ in range(snaps)]
    for at, part in zip(slots, parts):
        low = part[:depth, :]
        for snap in range(snaps):
            total[snap] = total[snap] + jnp.dot(
                slots_ref[at, snap], low, preferred_element_type=F32
            )
    return sum(total[snap] * time_ref[snap : snap + 1, :] for snap in range(snaps))


def first_kernel(slots, slots_ref, time_ref, *refs):
    parts, (result_ref, gram_ref) = refs[:-2], refs[-2:]
    result_ref[...] = multiply(slots, slots_ref, time_ref, parts)
    gram_ref[...] = gram_of(parts, slots_ref.shape[-1])


def last_kernel(slots, slots_ref, time_ref, result_ref, gram_ref, *refs):
    parts, (keep_ref, send_ref) = refs[:-2], refs[-2:]
    col, cols = lax.axis_index("col"), lax.axis_size("col")
    result = result_ref[...]
    if parts:
        result = result + multiply(slots, slots_ref, time_ref, parts)
    piece = result.shape[0] // cols
    core = lax.rem(col, 2)
    for pair in range(cols // 2):
        even = result[(2 * pair) * piece : (2 * pair + 1) * piece, :]
        odd = result[(2 * pair + 1) * piece : (2 * pair + 2) * piece, :]
        keep_ref[pair * piece : (pair + 1) * piece, :] = jnp.where(core == 0, even, odd)
        send_ref[pair * piece : (pair + 1) * piece, :] = jnp.where(core == 0, odd, even)
    send_ref[(cols // 2) * piece :, :] = gram_ref[...] + gram_of(parts, slots_ref.shape[-1])


def chip_kernel(piece, keep_ref, sent_ref, got_ref, gram_ref, *out_refs):
    held = keep_ref.shape[0]
    gram_ref[...] = sent_ref[held:, :] + got_ref[held:, :]
    place = lax.div(lax.axis_index("col"), 2)
    for offset, out_ref in enumerate(out_refs):
        start = pl.multiple_of(lax.bitwise_xor(place, offset) * piece, piece)
        out_ref[...] = keep_ref[pl.ds(start, piece), :] + got_ref[pl.ds(start, piece), :]


def negative_inverse(matrix):
    size = matrix.shape[0]
    tiles = BLOCK // TILE
    lane = lax.broadcasted_iota(jnp.int32, (TILE, size), 1)
    sub = lax.broadcasted_iota(jnp.int32, (TILE, size), 0)
    at_row = lax.broadcasted_iota(jnp.int32, (size, size), 0)
    at_col = lax.broadcasted_iota(jnp.int32, (size, size), 1)

    def spread(value, row):
        return jnp.broadcast_to(value[row : row + 1, :], (TILE, size))

    for begin in range(0, size, BLOCK):
        end = begin + BLOCK
        work = [matrix[begin + TILE * t : begin + TILE * (t + 1), :] for t in range(tiles)]
        solved = [None] * tiles
        for strip in range(0, BLOCK, STRIP):
            cols = [
                {
                    t: jnp.broadcast_to(work[t][:, at : at + 1], (TILE, size))
                    for t in range(strip // TILE, tiles)
                }
                for at in range(begin + strip, begin + strip + STRIP)
            ]
            for k in range(STRIP):
                tile, row = divmod(strip + k, TILE)
                scale = lax.rsqrt(spread(cols[k][tile], row))
                here = lane == begin + strip + k
                pivot = jnp.where(here, -1.0, spread(work[tile], row)) * scale
                solved[tile] = pivot if row == 0 else jnp.where(sub >= row, pivot, solved[tile])
                lower = {t: cols[k][t] * scale for t in range(tile, tiles)}
                lower[tile] = jnp.where(sub > row, lower[tile], 0.0)
                for j in range(k + 1, STRIP):
                    its_tile, its_row = divmod(strip + j, TILE)
                    if its_tile == tile:
                        factor = spread(cols[j][tile], row) * scale
                    else:
                        factor = spread(lower[its_tile], its_row)
                    for t in range(its_tile, tiles):
                        cols[j][t] = cols[j][t] - lower[t] * factor
                for t in range(tile, tiles):
                    work[t] = jnp.where(here, 0.0, work[t]) - lower[t] * pivot
        row_of = lax.broadcasted_iota(jnp.int32, (BLOCK, size), 0) + begin
        col_of = lax.broadcasted_iota(jnp.int32, (BLOCK, size), 1)
        upper = (col_of > row_of) & (col_of < end)
        hi, mid, lo = split3(jnp.where(upper, 0.0, jnp.concatenate(solved, 0)))
        update = tdot(
            jnp.concatenate([hi, hi, mid, mid, hi, lo], 0),
            jnp.concatenate([hi, mid, hi, mid, lo, hi], 0),
        )
        swept = (at_row >= begin) & (at_row < end) | (at_col >= begin) & (at_col < end)
        matrix = jnp.where(swept, 0.0, matrix) - update
    return matrix


def inverse_kernel(time_gram_ref, *refs):
    grams, inverse_ref = refs[:-1], refs[-1]
    gram = sum(ref[...] for ref in grams)
    inverse_ref[...] = negative_inverse(gram * time_gram_ref[...])


def solve_kernel(inverse_ref, *refs):
    sums, (solved_ref, squares_ref) = refs[:-2], refs[-2:]
    solved = -jnp.dot(
        sum(ref[...] for ref in sums),
        inverse_ref[...],
        precision=lax.Precision.HIGHEST,
        preferred_element_type=F32,
    )
    solved_ref[...] = solved
    squares = jnp.sum(solved * solved, axis=0, keepdims=True)
    squares_ref[...] = jnp.broadcast_to(squares, squares_ref.shape)


def shifted(value, axis, offset, groups):
    return lax.ppermute(value, axis, [(at, at ^ offset) for at in range(groups)])


def call(kernel, operands, in_specs, outs, scratch=()):
    return pl.pallas_call(
        kernel,
        out_shape=tuple(jax.ShapeDtypeStruct(shape, dtype) for shape, dtype in outs),
        in_specs=in_specs,
        out_specs=(VMEM,) * len(outs),
        scratch_shapes=scratch,
        compiler_params=pltpu.CompilerParams(vmem_limit_bytes=40 * 2**20),
    )(*operands)


def per_device(tensor, second_factor, time_factor):
    snaps, own_rows, own_cols = tensor.shape
    depth, rank = second_factor.shape
    rows, cols = lax.axis_size("row"), lax.axis_size("col")
    piece = own_rows // cols
    pairs = cols // 2

    whole = ((depth + rank, rank), BF16)
    message, own = call(prepare_kernel, (second_factor,), [VMEM], [whole, whole])
    passed = list(range(rows // 2 + rows // 2 % 2, rows, 2))
    forwarded = [at + 1 for at in passed]
    early = [at for at in range(rows) if at not in forwarded]
    arrived = {at: shifted(message, "row", at, rows) for at in early[1:]}
    arrived[0] = own
    direct = depth % 128 == 0
    owners, width = (early + forwarded, depth) if direct else ([0], own_cols)
    slots, time, time_gram = call(
        functools.partial(load_kernel, owners, width),
        (tensor, time_factor),
        [HBM, HBM],
        [((len(owners), snaps, own_rows, width), BF16), ((snaps, rank), F32), ((rank, rank), F32)],
        [pltpu.SemaphoreType.DMA((len(owners) + 1,))],
    )
    for at in passed:
        final = at == passed[-1]
        parts = [arrived[at]] + ([arrived[it] for it in passed[:-1]] if final else [])
        shape = whole if final else ((depth, rank), BF16)
        (relayed,) = call(relay_kernel, (time, *parts), [VMEM] * (1 + len(parts)), [shape])
        arrived[at + 1] = shifted(relayed, "row", 1, rows)
    if direct:
        first, last = [arrived[at] for at in early], [arrived[at] for at in forwarded]
    else:
        row = lax.axis_index("row")
        low = jnp.stack([arrived[at][:depth] for at in range(rows)])
        low = low[jnp.arange(rows) ^ row].reshape(rows * depth, rank)
        rests = [arrived[at][depth:].astype(F32) for at in early + forwarded[-1:]]
        first, last = [jnp.concatenate([low, sum(rests).astype(BF16)], 0)], []
    result, gram = call(
        functools.partial(first_kernel, range(len(first))),
        (slots, time, *first),
        [VMEM] * (2 + len(first)),
        [((own_rows, rank), F32), ((rank, rank), F32)],
    )
    keep, send = call(
        functools.partial(last_kernel, range(len(first), len(owners))),
        (slots, time, result, gram, *last),
        [VMEM] * (4 + len(last)),
        [((pairs * piece, rank), F32), ((pairs * piece + rank, rank), F32)],
    )

    chip_gram, own_sum, *outs = call(
        functools.partial(chip_kernel, piece),
        (keep, send, shifted(send, "col", 1, cols)),
        [VMEM] * 3,
        [((rank, rank), F32)] + [((piece, rank), F32)] * pairs,
    )
    grams = [chip_gram] + [shifted(chip_gram, "col", 2 * at, cols) for at in range(1, pairs)]
    sums = [own_sum] + [shifted(out, "col", 2 * (at + 1), cols) for at, out in enumerate(outs)]
    (inverse,) = call(
        inverse_kernel, (time_gram, *grams), [VMEM] * (1 + pairs), [((rank, rank), F32)]
    )
    solved, squares = call(
        solve_kernel,
        (inverse, *sums),
        [VMEM] * (1 + pairs),
        [((piece, rank), F32), ((rows * cols, rank), F32)],
    )
    squares = lax.all_to_all(squares, ("row", "col"), 0, 0, tiled=True)
    scales = jnp.sqrt(jnp.sum(squares, axis=0) / (own_rows * rows) + 1e-06)
    return solved / scales[None, :], scales


def solution(mesh):
    in_specs = (P(None, "row", "col"), P(("col", "row"), None), P())
    out_specs = (P(("row", "col"), None), P())
    return jax.shard_map(
        per_device, mesh=mesh, in_specs=in_specs, out_specs=out_specs, check_vma=False
    )
```

```python
import functools

import jax
import jax.numpy as jnp
from jax import lax
from jax.experimental import pallas as pl
from jax.experimental.pallas import tpu as pltpu
from jax.sharding import PartitionSpec as P

F32, BF16 = jnp.float32, jnp.bfloat16
HBM = pl.BlockSpec(memory_space=pltpu.HBM)
VMEM = pl.BlockSpec(memory_space=pltpu.VMEM)
TILE, STRIP, BLOCK = 8, 16, 32


def tdot(a, b):
    return lax.dot_general(a, b, (((0,), (0,)), ((), ())), preferred_element_type=F32)


def split3(x):
    hi = x.astype(BF16)
    rest = x - hi.astype(F32)
    mid = rest.astype(BF16)
    return hi, mid, (rest - mid.astype(F32)).astype(BF16)


def packed(square):
    size = square.shape[0]
    q, h = size // 4, size // 8
    return jnp.concatenate(
        [
            jnp.concatenate([square[2 * q : 3 * q, : 3 * q], square[:q, :q]], 1),
            square[3 * q :, :],
            jnp.concatenate([square[q : q + h, : 2 * q], square[q + h : 2 * q, : 2 * q]], 1),
        ],
        0,
    )


def unpacked(pack):
    size = pack.shape[1]
    q, h = size // 4, size // 8
    second = jnp.concatenate([pack[2 * q :, : 2 * q], pack[2 * q :, 2 * q :]], 0)
    lower = jnp.concatenate(
        [
            jnp.concatenate([pack[:q, 3 * q :], jnp.zeros((q, 3 * q), F32)], 1),
            jnp.concatenate([second, jnp.zeros((q, 2 * q), F32)], 1),
            jnp.concatenate([pack[:q, : 3 * q], jnp.zeros((q, q), F32)], 1),
            pack[q : 2 * q, :],
        ],
        0,
    )
    row = lax.broadcasted_iota(jnp.int32, (size, size), 0)
    col = lax.broadcasted_iota(jnp.int32, (size, size), 1)
    return jnp.where(col >= row, lower.T, lower)


def prepare_kernel(factor_ref, out_ref, own_ref):
    rows, rank = factor_ref.shape
    factor = factor_ref[...]
    low = factor.astype(BF16)
    residual = (factor - low.astype(F32)).astype(BF16)
    cross = tdot(low, residual)
    rest = packed((cross + cross.T + tdot(residual, residual)).astype(BF16))
    for ref in (out_ref, own_ref):
        ref[:rows, :] = low
        ref[rows:, :] = rest


def time_kernel(time_ref, out_ref, gram_ref):
    time = time_ref[...]
    out_ref[...] = time
    gram_ref[...] = lax.dot_general(
        time,
        time,
        (((0,), (0,)), ((), ())),
        precision=lax.Precision.HIGHEST,
        preferred_element_type=F32,
    )


def relay_kernel(ready_ref, part_ref, out_ref):
    del ready_ref
    out_ref[...] = part_ref[...]


def gram_of(parts, depth):
    gram, rest = 0.0, 0.0
    for part in parts:
        low = part[:depth, :]
        gram = gram + tdot(low, low)
        rest = rest + part[depth:, :].astype(F32)
    return gram, rest


def multiply(blocks, time_ref, parts, depth):
    snaps = time_ref.shape[0]
    total = [0.0] * snaps
    for (block, arrival), part in zip(blocks, parts):
        if arrival is not None:
            arrival.wait()
        low = part[:depth, :]
        for snap in range(snaps):
            total[snap] = total[snap] + jnp.dot(
                block[snap], low, preferred_element_type=F32
            )
    return sum(total[snap] * time_ref[snap : snap + 1, :] for snap in range(snaps))


def first_kernel(owners, depth, tensor_ref, time_ref, *refs):
    count = len(refs) - 6
    parts, (result_ref, gram_ref, rest_ref, later_ref, slots, sems) = refs[:count], refs[count:]
    row = lax.axis_index("row")
    blocks = []
    for at, owner in enumerate(owners):
        block = slots.at[at] if at < count else later_ref.at[at - count]
        start = pl.multiple_of(lax.bitwise_xor(row, owner) * depth, depth)
        arrival = pltpu.make_async_copy(
            tensor_ref.at[:, :, pl.ds(start, depth)], block, sems.at[at]
        )
        arrival.start()
        blocks.append((block, arrival))
    gram_ref[...], rest_ref[...] = gram_of(parts, depth)
    result_ref[...] = multiply(blocks[:count], time_ref, parts, depth)
    for _, arrival in blocks[count:]:
        arrival.wait()


def last_kernel(depth, time_ref, result_ref, gram_ref, rest_ref, *refs):
    parts, (later_ref, keep_ref, send_ref) = refs[:-3], refs[-3:]
    col, cols = lax.axis_index("col"), lax.axis_size("col")
    result = result_ref[...]
    gram, rest = gram_of(parts, depth)
    if parts:
        blocks = [(later_ref.at[at], None) for at in range(len(parts))]
        result = result + multiply(blocks, time_ref, parts, depth)
    piece = result.shape[0] // cols
    core = lax.rem(col, 2)
    for pair in range(cols // 2):
        even = result[(2 * pair) * piece : (2 * pair + 1) * piece, :]
        odd = result[(2 * pair + 1) * piece : (2 * pair + 2) * piece, :]
        keep_ref[pair * piece : (pair + 1) * piece, :] = jnp.where(core == 0, even, odd)
        send_ref[pair * piece : (pair + 1) * piece, :] = jnp.where(core == 0, odd, even)
    send_ref[(cols // 2) * piece :, :] = gram_ref[...] + gram + unpacked(rest_ref[...] + rest)


def chip_kernel(piece, keep_ref, sent_ref, got_ref, gram_ref, *out_refs):
    held = keep_ref.shape[0]
    gram_ref[...] = sent_ref[held:, :] + got_ref[held:, :]
    place = lax.div(lax.axis_index("col"), 2)
    for offset, out_ref in enumerate(out_refs):
        start = pl.multiple_of(lax.bitwise_xor(place, offset) * piece, piece)
        out_ref[...] = keep_ref[pl.ds(start, piece), :] + got_ref[pl.ds(start, piece), :]


def negative_inverse(matrix):
    size = matrix.shape[0]
    tiles = BLOCK // TILE
    lane = lax.broadcasted_iota(jnp.int32, (TILE, size), 1)
    sub = lax.broadcasted_iota(jnp.int32, (TILE, size), 0)
    at_row = lax.broadcasted_iota(jnp.int32, (size, size), 0)
    at_col = lax.broadcasted_iota(jnp.int32, (size, size), 1)

    def spread(value, row):
        return jnp.broadcast_to(value[row : row + 1, :], (TILE, size))

    for begin in range(0, size, BLOCK):
        end = begin + BLOCK
        work = [matrix[begin + TILE * t : begin + TILE * (t + 1), :] for t in range(tiles)]
        solved = [None] * tiles
        for strip in range(0, BLOCK, STRIP):
            cols = [
                {
                    t: jnp.broadcast_to(work[t][:, at : at + 1], (TILE, size))
                    for t in range(strip // TILE, tiles)
                }
                for at in range(begin + strip, begin + strip + STRIP)
            ]
            for k in range(STRIP):
                tile, row = divmod(strip + k, TILE)
                scale = lax.rsqrt(spread(cols[k][tile], row))
                here = lane == begin + strip + k
                pivot = jnp.where(here, -1.0, spread(work[tile], row)) * scale
                solved[tile] = pivot if row == 0 else jnp.where(sub >= row, pivot, solved[tile])
                lower = {t: cols[k][t] * scale for t in range(tile, tiles)}
                lower[tile] = jnp.where(sub > row, lower[tile], 0.0)
                for j in range(k + 1, STRIP):
                    its_tile, its_row = divmod(strip + j, TILE)
                    if its_tile == tile:
                        factor = spread(cols[j][tile], row) * scale
                    else:
                        factor = spread(lower[its_tile], its_row)
                    for t in range(its_tile, tiles):
                        cols[j][t] = cols[j][t] - lower[t] * factor
                for t in range(tile, tiles):
                    work[t] = jnp.where(here, 0.0, work[t]) - lower[t] * pivot
        row_of = lax.broadcasted_iota(jnp.int32, (BLOCK, size), 0) + begin
        col_of = lax.broadcasted_iota(jnp.int32, (BLOCK, size), 1)
        upper = (col_of > row_of) & (col_of < end)
        hi, mid, lo = split3(jnp.where(upper, 0.0, jnp.concatenate(solved, 0)))
        update = tdot(
            jnp.concatenate([hi, hi, mid, mid, hi, lo], 0),
            jnp.concatenate([hi, mid, hi, mid, lo, hi], 0),
        )
        swept = (at_row >= begin) & (at_row < end) | (at_col >= begin) & (at_col < end)
        matrix = jnp.where(swept, 0.0, matrix) - update
    return matrix


def inverse_kernel(time_gram_ref, *refs):
    grams, inverse_ref = refs[:-1], refs[-1]
    gram = sum(ref[...] for ref in grams)
    inverse_ref[...] = negative_inverse(gram * time_gram_ref[...])


def solve_kernel(inverse_ref, *refs):
    sums, (solved_ref, squares_ref) = refs[:-2], refs[-2:]
    solved = -jnp.dot(
        sum(ref[...] for ref in sums),
        inverse_ref[...],
        precision=lax.Precision.HIGHEST,
        preferred_element_type=F32,
    )
    solved_ref[...] = solved
    squares = jnp.sum(solved * solved, axis=0, keepdims=True)
    squares_ref[...] = jnp.broadcast_to(squares, squares_ref.shape)


def shifted(value, axis, offset, groups):
    return lax.ppermute(value, axis, [(at, at ^ offset) for at in range(groups)])


def call(kernel, operands, in_specs, outs, scratch=(), room=40):
    return pl.pallas_call(
        kernel,
        out_shape=tuple(jax.ShapeDtypeStruct(shape, dtype) for shape, dtype in outs),
        in_specs=in_specs,
        out_specs=(VMEM,) * len(outs),
        scratch_shapes=scratch,
        compiler_params=pltpu.CompilerParams(vmem_limit_bytes=room * 2**20),
    )(*operands)


def per_device(tensor, second_factor, time_factor):
    snaps, own_rows, own_cols = tensor.shape
    depth, rank = second_factor.shape
    rows, cols = lax.axis_size("row"), lax.axis_size("col")
    piece = own_rows // cols
    pairs = cols // 2

    pack = rank * 5 // 8
    whole = ((depth + pack, rank), BF16)
    message, own = call(prepare_kernel, (second_factor,), [VMEM], [whole, whole])
    half = rows // 2
    near = range(1, half)
    opposite = shifted(message, "row", half, rows)
    arrived = {at: shifted(message, "row", at, rows) for at in near}
    time, time_gram = call(
        time_kernel, (time_factor,), [VMEM], [((snaps, rank), F32), ((rank, rank), F32)]
    )
    (opposite,) = call(relay_kernel, (time, opposite), [VMEM] * 2, [whole])
    arrived[0], arrived[half] = own, opposite
    for at in near:
        arrived[half + at] = shifted(opposite, "row", at, rows)

    if depth % 128 == 0:
        owners, width, split = list(range(rows)), depth, half + 1
        parts = [arrived[at] for at in range(rows)]
    else:
        owners, width, split = [0], own_cols, 1
        row = lax.axis_index("row")
        low = jnp.stack([arrived[at][:depth] for at in range(rows)])
        low = low[jnp.arange(rows) ^ row].reshape(rows * depth, rank)
        rest = sum(arrived[at][depth:].astype(F32) for at in range(rows)).astype(BF16)
        parts = [jnp.concatenate([low, rest], 0)]
    square = ((rank, rank), F32)
    block = (snaps, own_rows, width)
    later = max(len(owners) - split, 1)
    result, gram, rest, tensor_later = call(
        functools.partial(first_kernel, owners, width),
        (tensor, time, *parts[:split]),
        [HBM] + [VMEM] * (1 + split),
        [((own_rows, rank), F32), square, ((pack, rank), F32), ((later, *block), BF16)],
        [pltpu.VMEM((split, *block), BF16), pltpu.SemaphoreType.DMA((len(owners),))],
        room=48,
    )
    keep, send = call(
        functools.partial(last_kernel, width),
        (time, result, gram, rest, *parts[split:], tensor_later),
        [VMEM] * (5 + len(parts) - split),
        [((pairs * piece, rank), F32), ((pairs * piece + rank, rank), F32)],
    )

    chip_gram, own_sum, *outs = call(
        functools.partial(chip_kernel, piece),
        (keep, send, shifted(send, "col", 1, cols)),
        [VMEM] * 3,
        [((rank, rank), F32)] + [((piece, rank), F32)] * pairs,
    )
    grams = [chip_gram] + [shifted(chip_gram, "col", 2 * at, cols) for at in range(1, pairs)]
    sums = [own_sum] + [shifted(out, "col", 2 * (at + 1), cols) for at, out in enumerate(outs)]
    (inverse,) = call(
        inverse_kernel, (time_gram, *grams), [VMEM] * (1 + pairs), [((rank, rank), F32)]
    )
    solved, squares = call(
        solve_kernel,
        (inverse, *sums),
        [VMEM] * (1 + pairs),
        [((piece, rank), F32), ((rows * cols, rank), F32)],
    )
    squares = lax.all_to_all(squares, ("row", "col"), 0, 0, tiled=True)
    scales = jnp.sqrt(jnp.sum(squares, axis=0) / (own_rows * rows) + 1e-06)
    return solved / scales[None, :], scales


def solution(mesh):
    in_specs = (P(None, "row", "col"), P(("col", "row"), None), P())
    out_specs = (P(("row", "col"), None), P())
    return jax.shard_map(
        per_device, mesh=mesh, in_specs=in_specs, out_specs=out_specs, check_vma=False
    )
```

```python
import functools

import jax
import jax.numpy as jnp
from jax import lax
from jax.experimental import pallas as pl
from jax.experimental.pallas import tpu as pltpu
from jax.sharding import PartitionSpec as P

F32, BF16 = jnp.float32, jnp.bfloat16
HBM = pl.BlockSpec(memory_space=pltpu.HBM)
VMEM = pl.BlockSpec(memory_space=pltpu.VMEM)
TILE, STRIP, BLOCK = 8, 16, 32


def tdot(a, b):
    return lax.dot_general(a, b, (((0,), (0,)), ((), ())), preferred_element_type=F32)


def split3(x):
    hi = x.astype(BF16)
    rest = x - hi.astype(F32)
    mid = rest.astype(BF16)
    return hi, mid, (rest - mid.astype(F32)).astype(BF16)


def packed(square):
    size = square.shape[0]
    q, h = size // 4, size // 8
    return jnp.concatenate(
        [
            jnp.concatenate([square[2 * q : 3 * q, : 3 * q], square[:q, :q]], 1),
            square[3 * q :, :],
            jnp.concatenate([square[q : q + h, : 2 * q], square[q + h : 2 * q, : 2 * q]], 1),
        ],
        0,
    )


def unpacked(pack):
    size = pack.shape[1]
    q, h = size // 4, size // 8
    second = jnp.concatenate([pack[2 * q :, : 2 * q], pack[2 * q :, 2 * q :]], 0)
    lower = jnp.concatenate(
        [
            jnp.concatenate([pack[:q, 3 * q :], jnp.zeros((q, 3 * q), F32)], 1),
            jnp.concatenate([second, jnp.zeros((q, 2 * q), F32)], 1),
            jnp.concatenate([pack[:q, : 3 * q], jnp.zeros((q, q), F32)], 1),
            pack[q : 2 * q, :],
        ],
        0,
    )
    row = lax.broadcasted_iota(jnp.int32, (size, size), 0)
    col = lax.broadcasted_iota(jnp.int32, (size, size), 1)
    return jnp.where(col >= row, lower.T, lower)


def prepare_kernel(factor_ref, out_ref, own_ref):
    rows, rank = factor_ref.shape
    factor = factor_ref[...]
    low = factor.astype(BF16)
    residual = (factor - low.astype(F32)).astype(BF16)
    cross = tdot(low, residual)
    rest = packed((cross + cross.T + tdot(residual, residual)).astype(BF16))
    for ref in (out_ref, own_ref):
        ref[:rows, :] = low
        ref[rows:, :] = rest


def start_loads(owners, depth, tensor_ref, slots_ref, sems):
    row = lax.axis_index("row")
    arrivals = []
    for at, owner in enumerate(owners):
        start = pl.multiple_of(lax.bitwise_xor(row, owner) * depth, depth)
        arrivals.append(
            pltpu.make_async_copy(
                tensor_ref.at[:, :, pl.ds(start, depth)], slots_ref.at[at], sems.at[at]
            )
        )
    for arrival in arrivals:
        arrival.start()
    return arrivals


def load_kernel(owners, depth, tensor_ref, time_ref, out_ref, gram_ref, slots_ref, sems):
    arrivals = start_loads(owners, depth, tensor_ref, slots_ref, sems)
    time = time_ref[...]
    out_ref[...] = time
    gram_ref[...] = lax.dot_general(
        time,
        time,
        (((0,), (0,)), ((), ())),
        precision=lax.Precision.HIGHEST,
        preferred_element_type=F32,
    )
    for arrival in arrivals:
        arrival.wait()


def relay_kernel(ready_ref, part_ref, out_ref):
    del ready_ref
    out_ref[...] = part_ref[...]


def gram_of(parts, depth):
    gram, rest = 0.0, 0.0
    for part in parts:
        low = part[:depth, :]
        gram = gram + tdot(low, low)
        rest = rest + part[depth:, :].astype(F32)
    return packed(gram) + rest


def multiply(blocks, time_ref, parts, depth):
    snaps = time_ref.shape[0]
    total = [0.0] * snaps
    for block, part in zip(blocks, parts):
        for snap in range(snaps):
            total[snap] = total[snap] + jnp.dot(
                block[snap], part[:depth, :], preferred_element_type=F32
            )
    return sum(total[snap] * time_ref[snap : snap + 1, :] for snap in range(snaps))


def first_kernel(owners, depth, tensor_ref, time_ref, early_ref, *refs):
    parts, (result_ref, gram_ref, later_ref, sems) = refs[:-4], refs[-4:]
    arrivals = start_loads(owners, depth, tensor_ref, later_ref, sems)
    begin = early_ref.shape[0]
    result_ref[...] = jnp.zeros(result_ref.shape, F32)

    @pl.loop(0, time_ref.shape[0])
    def _(snap):
        total = 0.0
        for at in range(begin):
            total = total + jnp.dot(
                early_ref[at, snap], parts[at][:depth, :], preferred_element_type=F32
            )
        result_ref[...] += total * time_ref[pl.ds(snap, 1), :]

    gram_ref[...] = gram_of(parts, depth)
    for at, arrival in enumerate(arrivals):
        arrival.wait()
        if begin + at < len(parts):
            result_ref[...] += multiply([later_ref.at[at]], time_ref, [parts[begin + at]], depth)


def middle_kernel(depth, places, time_ref, later_ref, result_ref, gram_ref, *refs):
    parts, (result_out_ref, gram_out_ref) = refs[:-2], refs[-2:]
    blocks = [later_ref.at[at] for at in places]
    result_out_ref[...] = result_ref[...] + multiply(blocks, time_ref, parts, depth)
    gram_out_ref[...] = gram_ref[...] + gram_of(parts, depth)


def last_kernel(depth, places, time_ref, later_ref, result_ref, gram_ref, *refs):
    parts, (keep_ref, send_ref) = refs[:-2], refs[-2:]
    col, cols = lax.axis_index("col"), lax.axis_size("col")
    result, gram = result_ref[...], gram_ref[...]
    if parts:
        blocks = [later_ref.at[at] for at in places]
        result = result + multiply(blocks, time_ref, parts, depth)
        gram = gram + gram_of(parts, depth)
    piece = result.shape[0] // cols
    core = lax.rem(col, 2)
    for pair in range(cols // 2):
        even = result[(2 * pair) * piece : (2 * pair + 1) * piece, :]
        odd = result[(2 * pair + 1) * piece : (2 * pair + 2) * piece, :]
        keep_ref[pair * piece : (pair + 1) * piece, :] = jnp.where(core == 0, even, odd)
        send_ref[pair * piece : (pair + 1) * piece, :] = jnp.where(core == 0, odd, even)
    send_ref[(cols // 2) * piece :, :] = gram


def chip_kernel(piece, keep_ref, sent_ref, got_ref, *out_refs):
    place = lax.div(lax.axis_index("col"), 2)
    held = keep_ref.shape[0]
    gram = sent_ref[held:, :] + got_ref[held:, :]
    for offset, out_ref in enumerate(out_refs):
        start = pl.multiple_of(lax.bitwise_xor(place, offset) * piece, piece)
        out_ref[:piece, :] = keep_ref[pl.ds(start, piece), :] + got_ref[pl.ds(start, piece), :]
        out_ref[piece:, :] = gram


def negative_inverse(matrix):
    size = matrix.shape[0]
    tiles = BLOCK // TILE
    lane = lax.broadcasted_iota(jnp.int32, (TILE, size), 1)
    sub = lax.broadcasted_iota(jnp.int32, (TILE, size), 0)
    at_row = lax.broadcasted_iota(jnp.int32, (size, size), 0)
    at_col = lax.broadcasted_iota(jnp.int32, (size, size), 1)

    def spread(value, row):
        return jnp.broadcast_to(value[row : row + 1, :], (TILE, size))

    for begin in range(0, size, BLOCK):
        end = begin + BLOCK
        work = [matrix[begin + TILE * t : begin + TILE * (t + 1), :] for t in range(tiles)]
        solved = [None] * tiles
        for strip in range(0, BLOCK, STRIP):
            cols = [
                {
                    t: jnp.broadcast_to(work[t][:, at : at + 1], (TILE, size))
                    for t in range(strip // TILE, tiles)
                }
                for at in range(begin + strip, begin + strip + STRIP)
            ]
            for k in range(STRIP):
                tile, row = divmod(strip + k, TILE)
                scale = lax.rsqrt(spread(cols[k][tile], row))
                here = lane == begin + strip + k
                pivot = jnp.where(here, -1.0, spread(work[tile], row)) * scale
                solved[tile] = pivot if row == 0 else jnp.where(sub >= row, pivot, solved[tile])
                lower = {t: cols[k][t] * scale for t in range(tile, tiles)}
                lower[tile] = jnp.where(sub > row, lower[tile], 0.0)
                for j in range(k + 1, STRIP):
                    its_tile, its_row = divmod(strip + j, TILE)
                    if its_tile == tile:
                        factor = spread(cols[j][tile], row) * scale
                    else:
                        factor = spread(lower[its_tile], its_row)
                    for t in range(its_tile, tiles):
                        cols[j][t] = cols[j][t] - lower[t] * factor
                for t in range(tile, tiles):
                    work[t] = jnp.where(here, 0.0, work[t]) - lower[t] * pivot
        row_of = lax.broadcasted_iota(jnp.int32, (BLOCK, size), 0) + begin
        col_of = lax.broadcasted_iota(jnp.int32, (BLOCK, size), 1)
        upper = (col_of > row_of) & (col_of < end)
        hi, mid, lo = split3(jnp.where(upper, 0.0, jnp.concatenate(solved, 0)))
        update = tdot(
            jnp.concatenate([hi, hi, mid, mid, hi, lo], 0),
            jnp.concatenate([hi, mid, hi, mid, lo, hi], 0),
        )
        swept = (at_row >= begin) & (at_row < end) | (at_col >= begin) & (at_col < end)
        matrix = jnp.where(swept, 0.0, matrix) - update
    return matrix


def solve_kernel(time_gram_ref, *refs):
    sums, (solved_ref, squares_ref) = refs[:-2], refs[-2:]
    piece = solved_ref.shape[0]
    total = sum(ref[...] for ref in sums)
    inverse = negative_inverse(unpacked(total[piece:, :]) * time_gram_ref[...])
    solved = -jnp.dot(
        total[:piece, :],
        inverse,
        precision=lax.Precision.HIGHEST,
        preferred_element_type=F32,
    )
    solved_ref[...] = solved
    squares = jnp.sum(solved * solved, axis=0, keepdims=True)
    squares_ref[...] = jnp.broadcast_to(squares, squares_ref.shape)


def shifted(value, axis, offset, groups):
    return lax.ppermute(value, axis, [(at, at ^ offset) for at in range(groups)])


def call(kernel, operands, in_specs, outs, scratch=(), room=24):
    return pl.pallas_call(
        kernel,
        out_shape=tuple(jax.ShapeDtypeStruct(shape, dtype) for shape, dtype in outs),
        in_specs=in_specs,
        out_specs=(VMEM,) * len(outs),
        scratch_shapes=scratch,
        compiler_params=pltpu.CompilerParams(vmem_limit_bytes=room * 2**20),
    )(*operands)


def per_device(tensor, second_factor, time_factor):
    snaps, own_rows, own_cols = tensor.shape
    depth, rank = second_factor.shape
    rows, cols = lax.axis_size("row"), lax.axis_size("col")
    piece = own_rows // cols
    pairs = cols // 2

    pack = rank * 5 // 8
    whole = ((depth + pack, rank), BF16)
    message, own = call(prepare_kernel, (second_factor,), [VMEM], [whole, whole])
    half = rows // 2
    near = range(1, half)
    opposite = shifted(message, "row", half, rows)
    arrived = {at: shifted(message, "row", at, rows) for at in near}
    in_hbm = pltpu.with_memory_space_constraint(tensor, pltpu.HBM)
    direct = depth % 128 == 0
    owners, width = (list(range(rows)), depth) if direct else ([0], own_cols)
    block = (snaps, own_rows, width)
    begin, split = (half, half + 1) if direct else (1, 1)
    time, time_gram, early = call(
        functools.partial(load_kernel, owners[:begin], width),
        (in_hbm, time_factor),
        [HBM, VMEM],
        [((snaps, rank), F32), ((rank, rank), F32), ((begin, *block), BF16)],
        [pltpu.SemaphoreType.DMA((begin,))],
    )
    (opposite,) = call(relay_kernel, (time, opposite), [VMEM] * 2, [whole])
    arrived[0], arrived[half] = own, opposite
    for at in near:
        arrived[half + at] = shifted(opposite, "row", at, rows)

    if direct:
        parts = [arrived[at] for at in range(rows)]
    else:
        row = lax.axis_index("row")
        low = jnp.stack([arrived[at][:depth] for at in range(rows)])
        low = low[jnp.arange(rows) ^ row].reshape(rows * depth, rank)
        rest = sum(arrived[at][depth:].astype(F32) for at in range(rows)).astype(BF16)
        parts = [jnp.concatenate([low, rest], 0)]
    later = max(len(owners) - begin, 1)
    sums = [((own_rows, rank), F32), ((pack, rank), F32)]
    result, gram, tensor_later = call(
        functools.partial(first_kernel, owners[begin:], width),
        (in_hbm, time, early, *parts[:split]),
        [HBM] + [VMEM] * (2 + split),
        sums + [((later, *block), BF16)],
        [pltpu.SemaphoreType.DMA((later,))],
    )
    if len(parts) > split + 1:
        middle = parts[split:-1]
        result, gram = call(
            functools.partial(middle_kernel, width, range(split - begin, later - 1)),
            (time, tensor_later, result, gram, *middle),
            [VMEM] * (4 + len(middle)),
            sums,
        )
    last = parts[split:][-1:]
    keep, send = call(
        functools.partial(last_kernel, width, [later - 1]),
        (time, tensor_later, result, gram, *last),
        [VMEM] * (4 + len(last)),
        [((pairs * piece, rank), F32), ((pairs * piece + pack, rank), F32)],
    )

    total, *outs = call(
        functools.partial(chip_kernel, piece),
        (keep, send, shifted(send, "col", 1, cols)),
        [VMEM] * 3,
        [((piece + pack, rank), F32)] * pairs,
    )
    totals = [total] + [shifted(out, "col", 2 * (at + 1), cols) for at, out in enumerate(outs)]
    solved, squares = call(
        solve_kernel,
        (time_gram, *totals),
        [VMEM] * (1 + pairs),
        [((piece, rank), F32), ((rows * cols, rank), F32)],
    )
    squares = lax.all_to_all(squares, ("row", "col"), 0, 0, tiled=True)
    scales = jnp.sqrt(jnp.sum(squares, axis=0) / (own_rows * rows) + 1e-06)
    return solved / scales[None, :], scales


def solution(mesh):
    in_specs = (P(None, "row", "col"), P(("col", "row"), None), P())
    out_specs = (P(("row", "col"), None), P())
    return jax.shard_map(
        per_device, mesh=mesh, in_specs=in_specs, out_specs=out_specs, check_vma=False
    )
```

```python
import functools

import jax
import jax.numpy as jnp
from jax import lax
from jax.experimental import pallas as pl
from jax.experimental.pallas import tpu as pltpu
from jax.sharding import PartitionSpec as P

F32, BF16 = jnp.float32, jnp.bfloat16
HBM = pl.BlockSpec(memory_space=pltpu.HBM)
VMEM = pl.BlockSpec(memory_space=pltpu.VMEM)
TILE, STRIP, BLOCK = 8, 16, 32


def tdot(a, b):
    return lax.dot_general(a, b, (((0,), (0,)), ((), ())), preferred_element_type=F32)


def split3(x):
    hi = x.astype(BF16)
    rest = x - hi.astype(F32)
    mid = rest.astype(BF16)
    return hi, mid, (rest - mid.astype(F32)).astype(BF16)


def packed(square):
    size = square.shape[0]
    q, h = size // 4, size // 8
    return jnp.concatenate(
        [
            jnp.concatenate([square[2 * q : 3 * q, : 3 * q], square[:q, :q]], 1),
            square[3 * q :, :],
            jnp.concatenate([square[q : q + h, : 2 * q], square[q + h : 2 * q, : 2 * q]], 1),
        ],
        0,
    )


def unpacked(pack):
    size = pack.shape[1]
    q, h = size // 4, size // 8
    second = jnp.concatenate([pack[2 * q :, : 2 * q], pack[2 * q :, 2 * q :]], 0)
    lower = jnp.concatenate(
        [
            jnp.concatenate([pack[:q, 3 * q :], jnp.zeros((q, 3 * q), F32)], 1),
            jnp.concatenate([second, jnp.zeros((q, 2 * q), F32)], 1),
            jnp.concatenate([pack[:q, : 3 * q], jnp.zeros((q, q), F32)], 1),
            pack[q : 2 * q, :],
        ],
        0,
    )
    row = lax.broadcasted_iota(jnp.int32, (size, size), 0)
    col = lax.broadcasted_iota(jnp.int32, (size, size), 1)
    return jnp.where(col >= row, lower.T, lower)


def prepare_kernel(factor_ref, out_ref, own_ref):
    rows, rank = factor_ref.shape
    factor = factor_ref[...]
    low = factor.astype(BF16)
    residual = (factor - low.astype(F32)).astype(BF16)
    cross = tdot(low, residual)
    rest = packed((cross + cross.T + tdot(residual, residual)).astype(BF16))
    for ref in (out_ref, own_ref):
        ref[:rows, :] = low
        ref[rows:, :] = rest


def start_loads(owners, depth, tensor_ref, slots_ref, sems):
    row = lax.axis_index("row")
    arrivals = []
    for at, owner in enumerate(owners):
        start = pl.multiple_of(lax.bitwise_xor(row, owner) * depth, depth)
        arrivals.append(
            pltpu.make_async_copy(
                tensor_ref.at[:, :, pl.ds(start, depth)], slots_ref.at[at], sems.at[at]
            )
        )
    for arrival in arrivals:
        arrival.start()
    return arrivals


def load_kernel(owners, depth, tensor_ref, time_ref, out_ref, gram_ref, slots_ref, sems):
    time_arrival = pltpu.make_async_copy(time_ref, out_ref, sems.at[len(owners)])
    time_arrival.start()
    arrivals = start_loads(owners, depth, tensor_ref, slots_ref, sems)
    time_arrival.wait()
    time = out_ref[...]
    gram_ref[...] = lax.dot_general(
        time,
        time,
        (((0,), (0,)), ((), ())),
        precision=lax.Precision.HIGHEST,
        preferred_element_type=F32,
    )
    for arrival in arrivals:
        arrival.wait()


def relay_kernel(ready_ref, part_ref, out_ref):
    del ready_ref
    out_ref[...] = part_ref[...]


def gram_of(parts, depth):
    gram, rest = 0.0, 0.0
    for part in parts:
        low = part[:depth, :]
        gram = gram + tdot(low, low)
        rest = rest + part[depth:, :].astype(F32)
    return packed(gram) + rest


def multiply(blocks, time_ref, parts, depth):
    snaps = time_ref.shape[0]
    total = [0.0] * snaps
    for block, part in zip(blocks, parts):
        for snap in range(snaps):
            total[snap] = total[snap] + jnp.dot(
                block[snap], part[:depth, :], preferred_element_type=F32
            )
    return sum(total[snap] * time_ref[snap : snap + 1, :] for snap in range(snaps))


def first_kernel(owners, depth, tensor_ref, time_ref, early_ref, *refs):
    parts, (result_ref, gram_ref, later_ref, sems) = refs[:-4], refs[-4:]
    arrivals = start_loads(owners, depth, tensor_ref, later_ref, sems)
    result_ref[...] = jnp.zeros(result_ref.shape, F32)

    @pl.loop(0, time_ref.shape[0])
    def _(snap):
        total = 0.0
        for at, part in enumerate(parts):
            total = total + jnp.dot(
                early_ref[at, snap], part[:depth, :], preferred_element_type=F32
            )
        result_ref[...] += total * time_ref[pl.ds(snap, 1), :]

    gram_ref[...] = gram_of(parts, depth)
    for arrival in arrivals:
        arrival.wait()


def last_kernel(depth, time_ref, early_ref, later_ref, result_ref, gram_ref, *refs):
    parts, (keep_ref, send_ref) = refs[:-2], refs[-2:]
    col, cols = lax.axis_index("col"), lax.axis_size("col")
    result, gram = result_ref[...], gram_ref[...]
    if parts:
        begin, later = early_ref.shape[0], later_ref.shape[0]
        blocks = [early_ref.at[at] for at in range(begin)]
        blocks = (blocks + [later_ref.at[at] for at in range(later)])[-len(parts) :]
        result = result + multiply(blocks, time_ref, parts, depth)
        gram = gram + gram_of(parts, depth)
    piece = result.shape[0] // cols
    core = lax.rem(col, 2)
    for pair in range(cols // 2):
        even = result[(2 * pair) * piece : (2 * pair + 1) * piece, :]
        odd = result[(2 * pair + 1) * piece : (2 * pair + 2) * piece, :]
        keep_ref[pair * piece : (pair + 1) * piece, :] = jnp.where(core == 0, even, odd)
        send_ref[pair * piece : (pair + 1) * piece, :] = jnp.where(core == 0, odd, even)
    send_ref[(cols // 2) * piece :, :] = gram


def chip_kernel(piece, keep_ref, sent_ref, got_ref, gram_ref, *out_refs):
    place = lax.div(lax.axis_index("col"), 2)
    held = keep_ref.shape[0]
    gram_ref[...] = sent_ref[held:, :] + got_ref[held:, :]
    for offset, out_ref in enumerate(out_refs):
        start = pl.multiple_of(lax.bitwise_xor(place, offset) * piece, piece)
        out_ref[...] = keep_ref[pl.ds(start, piece), :] + got_ref[pl.ds(start, piece), :]


def negative_inverse(matrix):
    size = matrix.shape[0]
    tiles = BLOCK // TILE
    lane = lax.broadcasted_iota(jnp.int32, (TILE, size), 1)
    sub = lax.broadcasted_iota(jnp.int32, (TILE, size), 0)
    at_row = lax.broadcasted_iota(jnp.int32, (size, size), 0)
    at_col = lax.broadcasted_iota(jnp.int32, (size, size), 1)

    def spread(value, row):
        return jnp.broadcast_to(value[row : row + 1, :], (TILE, size))

    for begin in range(0, size, BLOCK):
        end = begin + BLOCK
        work = [matrix[begin + TILE * t : begin + TILE * (t + 1), :] for t in range(tiles)]
        solved = [None] * tiles
        for strip in range(0, BLOCK, STRIP):
            cols = [
                {
                    t: jnp.broadcast_to(work[t][:, at : at + 1], (TILE, size))
                    for t in range(strip // TILE, tiles)
                }
                for at in range(begin + strip, begin + strip + STRIP)
            ]
            for k in range(STRIP):
                tile, row = divmod(strip + k, TILE)
                scale = lax.rsqrt(spread(cols[k][tile], row))
                here = lane == begin + strip + k
                pivot = jnp.where(here, -1.0, spread(work[tile], row)) * scale
                solved[tile] = pivot if row == 0 else jnp.where(sub >= row, pivot, solved[tile])
                lower = {t: cols[k][t] * scale for t in range(tile, tiles)}
                lower[tile] = jnp.where(sub > row, lower[tile], 0.0)
                for j in range(k + 1, STRIP):
                    its_tile, its_row = divmod(strip + j, TILE)
                    if its_tile == tile:
                        factor = spread(cols[j][tile], row) * scale
                    else:
                        factor = spread(lower[its_tile], its_row)
                    for t in range(its_tile, tiles):
                        cols[j][t] = cols[j][t] - lower[t] * factor
                for t in range(tile, tiles):
                    work[t] = jnp.where(here, 0.0, work[t]) - lower[t] * pivot
        row_of = lax.broadcasted_iota(jnp.int32, (BLOCK, size), 0) + begin
        col_of = lax.broadcasted_iota(jnp.int32, (BLOCK, size), 1)
        upper = (col_of > row_of) & (col_of < end)
        hi, mid, lo = split3(jnp.where(upper, 0.0, jnp.concatenate(solved, 0)))
        update = tdot(
            jnp.concatenate([hi, hi, mid, mid, hi, lo], 0),
            jnp.concatenate([hi, mid, hi, mid, lo, hi], 0),
        )
        swept = (at_row >= begin) & (at_row < end) | (at_col >= begin) & (at_col < end)
        matrix = jnp.where(swept, 0.0, matrix) - update
    return matrix


def inverse_kernel(time_gram_ref, *refs):
    grams, inverse_ref = refs[:-1], refs[-1]
    gram = unpacked(sum(ref[...] for ref in grams))
    inverse_ref[...] = negative_inverse(gram * time_gram_ref[...])


def solve_kernel(inverse_ref, *refs):
    sums, (solved_ref, squares_ref) = refs[:-2], refs[-2:]
    solved = -jnp.dot(
        sum(ref[...] for ref in sums),
        inverse_ref[...],
        precision=lax.Precision.HIGHEST,
        preferred_element_type=F32,
    )
    solved_ref[...] = solved
    squares = jnp.sum(solved * solved, axis=0, keepdims=True)
    squares_ref[...] = jnp.broadcast_to(squares, squares_ref.shape)


def shifted(value, axis, offset, groups):
    return lax.ppermute(value, axis, [(at, at ^ offset) for at in range(groups)])


def call(kernel, operands, in_specs, outs, scratch=(), room=24, flops=0):
    return pl.pallas_call(
        kernel,
        out_shape=tuple(jax.ShapeDtypeStruct(shape, dtype) for shape, dtype in outs),
        in_specs=in_specs,
        out_specs=(VMEM,) * len(outs),
        scratch_shapes=scratch,
        cost_estimate=pl.CostEstimate(flops=flops, bytes_accessed=0, transcendentals=0) if flops else None,
        compiler_params=pltpu.CompilerParams(vmem_limit_bytes=room * 2**20),
    )(*operands)


def per_device(tensor, second_factor, time_factor):
    snaps, own_rows, own_cols = tensor.shape
    depth, rank = second_factor.shape
    rows, cols = lax.axis_size("row"), lax.axis_size("col")
    piece = own_rows // cols
    pairs = cols // 2

    pack = rank * 5 // 8
    whole = ((depth + pack, rank), BF16)
    message, own = call(prepare_kernel, (second_factor,), [VMEM], [whole, whole])
    half = rows // 2
    near = sorted(range(1, half), key=lambda at: (bin(at).count("0") - len(bin(at)), at))
    opposite = shifted(message, "row", half, rows)
    arrived = {at: shifted(message, "row", at, rows) for at in near}
    in_hbm = pltpu.with_memory_space_constraint(tensor, pltpu.HBM)
    direct = depth % 128 == 0
    owners, width = ([0, *near, half, *(half + at for at in near)], depth) if direct else ([0], own_cols)
    block = (snaps, own_rows, width)
    begin, split = (half + 1, half + 1) if direct else (1, 1)
    time, time_gram, early = call(
        functools.partial(load_kernel, owners[:begin], width),
        (in_hbm, pltpu.with_memory_space_constraint(time_factor, pltpu.HBM)),
        [HBM, HBM],
        [((snaps, rank), F32), ((rank, rank), F32), ((begin, *block), BF16)],
        [pltpu.SemaphoreType.DMA((begin + 1,))],
    )
    (opposite,) = call(relay_kernel, (time, opposite), [VMEM] * 2, [whole])
    arrived[0], arrived[half] = own, opposite
    for at in near:
        arrived[half + at] = shifted(opposite, "row", at, rows)

    if direct:
        parts = [arrived[at] for at in owners]
    else:
        row = lax.axis_index("row")
        low = jnp.stack([arrived[at][:depth] for at in range(rows)])
        low = low[jnp.arange(rows) ^ row].reshape(rows * depth, rank)
        rest = sum(arrived[at][depth:].astype(F32) for at in range(rows)).astype(BF16)
        parts = [jnp.concatenate([low, rest], 0)]
    later = max(len(owners) - begin, 1)
    sums = [((own_rows, rank), F32), ((pack, rank), F32)]
    result, gram, tensor_later = call(
        functools.partial(first_kernel, owners[begin:], width),
        (in_hbm, time, early, *parts[:split]),
        [HBM] + [VMEM] * (2 + split),
        sums + [((later, *block), BF16)],
        [pltpu.SemaphoreType.DMA((later,))],
    )
    last = parts[split:]
    keep, send = call(
        functools.partial(last_kernel, width),
        (time, early, tensor_later, result, gram, *last),
        [VMEM] * (5 + len(last)),
        [((pairs * piece, rank), F32), ((pairs * piece + pack, rank), F32)],
    )

    chip_gram, own_sum, *outs = call(
        functools.partial(chip_kernel, piece),
        (keep, send, shifted(send, "col", 1, cols)),
        [VMEM] * 3,
        [((pack, rank), F32)] + [((piece, rank), F32)] * pairs,
    )
    grams = [chip_gram] + [shifted(chip_gram, "col", 2 * at, cols) for at in range(1, pairs)]
    pieces = [own_sum] + [shifted(out, "col", 2 * (at + 1), cols) for at, out in enumerate(outs)]
    (inverse,) = call(
        inverse_kernel, (time_gram, *grams), [VMEM] * (1 + pairs), [((rank, rank), F32)], flops=2 * 10**9
    )
    solved, squares = call(
        solve_kernel,
        (inverse, *pieces),
        [VMEM] * (1 + pairs),
        [((piece, rank), F32), ((rows * cols, rank), F32)],
    )
    squares = lax.all_to_all(squares, ("row", "col"), 0, 0, tiled=True)
    scales = jnp.sqrt(jnp.sum(squares, axis=0) / (own_rows * rows) + 1e-06)
    return solved / scales[None, :], scales


def solution(mesh):
    in_specs = (P(None, "row", "col"), P(("col", "row"), None), P())
    out_specs = (P(("row", "col"), None), P())
    return jax.shard_map(
        per_device, mesh=mesh, in_specs=in_specs, out_specs=out_specs, check_vma=False
    )
```

```python
import functools

import jax
import jax.numpy as jnp
from jax import lax
from jax.experimental import pallas as pl
from jax.experimental.pallas import tpu as pltpu
from jax.sharding import PartitionSpec as P

F32, BF16 = jnp.float32, jnp.bfloat16
HBM = pl.BlockSpec(memory_space=pltpu.HBM)
VMEM = pl.BlockSpec(memory_space=pltpu.VMEM)
TILE, STRIP, BLOCK = 8, 16, 32


def tdot(a, b):
    return lax.dot_general(a, b, (((0,), (0,)), ((), ())), preferred_element_type=F32)


def split3(x):
    hi = x.astype(BF16)
    rest = x - hi.astype(F32)
    mid = rest.astype(BF16)
    return hi, mid, (rest - mid.astype(F32)).astype(BF16)


def packed(square):
    size = square.shape[0]
    q, h = size // 4, size // 8
    return jnp.concatenate(
        [
            jnp.concatenate([square[2 * q : 3 * q, : 3 * q], square[:q, :q]], 1),
            square[3 * q :, :],
            jnp.concatenate([square[q : q + h, : 2 * q], square[q + h : 2 * q, : 2 * q]], 1),
        ],
        0,
    )


def unpacked(pack):
    size = pack.shape[1]
    q, h = size // 4, size // 8
    second = jnp.concatenate([pack[2 * q :, : 2 * q], pack[2 * q :, 2 * q :]], 0)
    lower = jnp.concatenate(
        [
            jnp.concatenate([pack[:q, 3 * q :], jnp.zeros((q, 3 * q), F32)], 1),
            jnp.concatenate([second, jnp.zeros((q, 2 * q), F32)], 1),
            jnp.concatenate([pack[:q, : 3 * q], jnp.zeros((q, q), F32)], 1),
            pack[q : 2 * q, :],
        ],
        0,
    )
    row = lax.broadcasted_iota(jnp.int32, (size, size), 0)
    col = lax.broadcasted_iota(jnp.int32, (size, size), 1)
    return jnp.where(col >= row, lower.T, lower)


def prepare_kernel(factor_ref, out_ref, own_ref):
    rows, rank = factor_ref.shape
    factor = factor_ref[...]
    low = factor.astype(BF16)
    residual = (factor - low.astype(F32)).astype(BF16)
    cross = tdot(low, residual)
    rest = packed((cross + cross.T + tdot(residual, residual)).astype(BF16))
    for ref in (out_ref, own_ref):
        ref[:rows, :] = low
        ref[rows:, :] = rest


def start_loads(owners, depth, tensor_ref, slots_ref, sems):
    row = lax.axis_index("row")
    arrivals = []
    for at, owner in enumerate(owners):
        start = pl.multiple_of(lax.bitwise_xor(row, owner) * depth, depth)
        arrivals.append(
            pltpu.make_async_copy(
                tensor_ref.at[:, :, pl.ds(start, depth)], slots_ref.at[at], sems.at[at]
            )
        )
    for arrival in arrivals:
        arrival.start()
    return arrivals


def load_kernel(owners, depth, tensor_ref, time_ref, out_ref, gram_ref, slots_ref, sems):
    time_arrival = pltpu.make_async_copy(time_ref, out_ref, sems.at[len(owners)])
    time_arrival.start()
    arrivals = start_loads(owners, depth, tensor_ref, slots_ref, sems)
    time_arrival.wait()
    time = out_ref[...]
    gram_ref[...] = lax.dot_general(
        time,
        time,
        (((0,), (0,)), ((), ())),
        precision=lax.Precision.HIGHEST,
        preferred_element_type=F32,
    )
    for arrival in arrivals:
        arrival.wait()


def relay_kernel(ready_ref, part_ref, out_ref):
    del ready_ref
    out_ref[...] = part_ref[...]


def gram_of(parts, depth):
    gram, rest = 0.0, 0.0
    for part in parts:
        low = part[:depth, :]
        gram = gram + tdot(low, low)
        rest = rest + part[depth:, :].astype(F32)
    return packed(gram) + rest


def first_kernel(owners, depth, tensor_ref, time_ref, early_ref, *refs):
    parts, (result_ref, gram_ref, later_ref, sems) = refs[:-4], refs[-4:]
    arrivals = start_loads(owners, depth, tensor_ref, later_ref, sems)
    result_ref[...] = jnp.zeros(result_ref.shape, F32)

    @pl.loop(0, time_ref.shape[0])
    def _(snap):
        total = 0.0
        for at, part in enumerate(parts):
            total = total + jnp.dot(
                early_ref[at, snap], part[:depth, :], preferred_element_type=F32
            )
        result_ref[...] += total * time_ref[pl.ds(snap, 1), :]

    gram_ref[...] = gram_of(parts, depth)
    for arrival in arrivals:
        arrival.wait()


def last_kernel(depth, other, time_ref, early_ref, later_ref, result_ref, gram_ref, *refs):
    parts, out_ref = refs[:-1], refs[-1]
    col, cols = lax.axis_index("col"), lax.axis_size("col")
    piece = result_ref.shape[0] // cols
    side = lax.rem(col + other, 2)
    begin, later = early_ref.shape[0], later_ref.shape[0]
    blocks = [early_ref.at[at] for at in range(begin)]
    blocks = (blocks + [later_ref.at[at] for at in range(later)])[begin + later - len(parts) :]
    for pair in range(cols // 2):
        rows = pl.ds(pl.multiple_of((2 * pair + side) * piece, piece), piece)
        total = result_ref[rows, :]
        for snap in range(time_ref.shape[0] if parts else 0):
            product = sum(
                jnp.dot(block[snap, rows, :], part[:depth, :], preferred_element_type=F32)
                for block, part in zip(blocks, parts)
            )
            total = total + product * time_ref[snap : snap + 1, :]
        out_ref[pair * piece : (pair + 1) * piece, :] = total
    if other:
        gram = gram_ref[...]
        if parts:
            gram = gram + gram_of(parts, depth)
        out_ref[(cols // 2) * piece :, :] = gram


def chip_kernel(piece, keep_ref, sent_ref, got_ref, gram_ref, *out_refs):
    place = lax.div(lax.axis_index("col"), 2)
    held = keep_ref.shape[0]
    gram_ref[...] = sent_ref[held:, :] + got_ref[held:, :]
    for offset, out_ref in enumerate(out_refs):
        start = pl.multiple_of(lax.bitwise_xor(place, offset) * piece, piece)
        out_ref[...] = keep_ref[pl.ds(start, piece), :] + got_ref[pl.ds(start, piece), :]


def negative_inverse(matrix):
    size = matrix.shape[0]
    tiles = BLOCK // TILE
    lane = lax.broadcasted_iota(jnp.int32, (TILE, size), 1)
    sub = lax.broadcasted_iota(jnp.int32, (TILE, size), 0)
    at_row = lax.broadcasted_iota(jnp.int32, (size, size), 0)
    at_col = lax.broadcasted_iota(jnp.int32, (size, size), 1)

    def spread(value, row):
        return jnp.broadcast_to(value[row : row + 1, :], (TILE, size))

    for begin in range(0, size, BLOCK):
        end = begin + BLOCK
        work = [matrix[begin + TILE * t : begin + TILE * (t + 1), :] for t in range(tiles)]
        solved = [None] * tiles
        for strip in range(0, BLOCK, STRIP):
            cols = [
                {
                    t: jnp.broadcast_to(work[t][:, at : at + 1], (TILE, size))
                    for t in range(strip // TILE, tiles)
                }
                for at in range(begin + strip, begin + strip + STRIP)
            ]
            for k in range(STRIP):
                tile, row = divmod(strip + k, TILE)
                scale = lax.rsqrt(spread(cols[k][tile], row))
                here = lane == begin + strip + k
                pivot = jnp.where(here, -1.0, spread(work[tile], row)) * scale
                solved[tile] = pivot if row == 0 else jnp.where(sub >= row, pivot, solved[tile])
                lower = {t: cols[k][t] * scale for t in range(tile, tiles)}
                lower[tile] = jnp.where(sub > row, lower[tile], 0.0)
                for j in range(k + 1, STRIP):
                    its_tile, its_row = divmod(strip + j, TILE)
                    if its_tile == tile:
                        factor = spread(cols[j][tile], row) * scale
                    else:
                        factor = spread(lower[its_tile], its_row)
                    for t in range(its_tile, tiles):
                        cols[j][t] = cols[j][t] - lower[t] * factor
                for t in range(tile, tiles):
                    work[t] = jnp.where(here, 0.0, work[t]) - lower[t] * pivot
        row_of = lax.broadcasted_iota(jnp.int32, (BLOCK, size), 0) + begin
        col_of = lax.broadcasted_iota(jnp.int32, (BLOCK, size), 1)
        upper = (col_of > row_of) & (col_of < end)
        hi, mid, lo = split3(jnp.where(upper, 0.0, jnp.concatenate(solved, 0)))
        update = tdot(
            jnp.concatenate([hi, hi, mid, mid, hi, lo], 0),
            jnp.concatenate([hi, mid, hi, mid, lo, hi], 0),
        )
        swept = (at_row >= begin) & (at_row < end) | (at_col >= begin) & (at_col < end)
        matrix = jnp.where(swept, 0.0, matrix) - update
    return matrix


def inverse_kernel(time_gram_ref, *refs):
    grams, inverse_ref = refs[:-1], refs[-1]
    gram = unpacked(sum(ref[...] for ref in grams))
    inverse_ref[...] = negative_inverse(gram * time_gram_ref[...])


def solve_kernel(inverse_ref, *refs):
    sums, (solved_ref, squares_ref) = refs[:-2], refs[-2:]
    solved = -jnp.dot(
        sum(ref[...] for ref in sums),
        inverse_ref[...],
        precision=lax.Precision.HIGHEST,
        preferred_element_type=F32,
    )
    solved_ref[...] = solved
    squares = jnp.sum(solved * solved, axis=0, keepdims=True)
    squares_ref[...] = jnp.broadcast_to(squares, squares_ref.shape)


def shifted(value, axis, offset, groups):
    return lax.ppermute(value, axis, [(at, at ^ offset) for at in range(groups)])


def call(kernel, operands, in_specs, outs, scratch=(), room=24, flops=0):
    return pl.pallas_call(
        kernel,
        out_shape=tuple(jax.ShapeDtypeStruct(shape, dtype) for shape, dtype in outs),
        in_specs=in_specs,
        out_specs=(VMEM,) * len(outs),
        scratch_shapes=scratch,
        cost_estimate=pl.CostEstimate(flops=flops, bytes_accessed=0, transcendentals=0) if flops else None,
        compiler_params=pltpu.CompilerParams(vmem_limit_bytes=room * 2**20),
    )(*operands)


def per_device(tensor, second_factor, time_factor):
    snaps, own_rows, own_cols = tensor.shape
    depth, rank = second_factor.shape
    rows, cols = lax.axis_size("row"), lax.axis_size("col")
    piece = own_rows // cols
    pairs = cols // 2

    pack = rank * 5 // 8
    whole = ((depth + pack, rank), BF16)
    message, own = call(prepare_kernel, (second_factor,), [VMEM], [whole, whole])
    half = rows // 2
    near = sorted(range(1, half), key=lambda at: (bin(at).count("0") - len(bin(at)), at))
    opposite = shifted(message, "row", half, rows)
    arrived = {at: shifted(message, "row", at, rows) for at in near}
    in_hbm = pltpu.with_memory_space_constraint(tensor, pltpu.HBM)
    direct = depth % 128 == 0
    owners, width = ([0, *near, half, *(half + at for at in near)], depth) if direct else ([0], own_cols)
    block = (snaps, own_rows, width)
    begin, split = (half + 1, half + 1) if direct else (1, 1)
    time, time_gram, early = call(
        functools.partial(load_kernel, owners[:begin], width),
        (in_hbm, pltpu.with_memory_space_constraint(time_factor, pltpu.HBM)),
        [HBM, HBM],
        [((snaps, rank), F32), ((rank, rank), F32), ((begin, *block), BF16)],
        [pltpu.SemaphoreType.DMA((begin + 1,))],
    )
    (opposite,) = call(relay_kernel, (time, opposite), [VMEM] * 2, [whole])
    arrived[0], arrived[half] = own, opposite
    for at in near:
        arrived[half + at] = shifted(opposite, "row", at, rows)

    if direct:
        parts = [arrived[at] for at in owners]
    else:
        row = lax.axis_index("row")
        low = jnp.stack([arrived[at][:depth] for at in range(rows)])
        low = low[jnp.arange(rows) ^ row].reshape(rows * depth, rank)
        rest = sum(arrived[at][depth:].astype(F32) for at in range(rows)).astype(BF16)
        parts = [jnp.concatenate([low, rest], 0)]
    later = max(len(owners) - begin, 1)
    sums = [((own_rows, rank), F32), ((pack, rank), F32)]
    result, gram, tensor_later = call(
        functools.partial(first_kernel, owners[begin:], width),
        (in_hbm, time, early, *parts[:split]),
        [HBM] + [VMEM] * (2 + split),
        sums + [((later, *block), BF16)],
        [pltpu.SemaphoreType.DMA((later,))],
    )
    last = parts[split:]
    held = pairs * piece
    operands = (time, early, tensor_later, result, gram, *last)
    specs = [VMEM] * len(operands)
    other, own = functools.partial(last_kernel, width, 1), functools.partial(last_kernel, width, 0)
    (send,) = call(other, operands, specs, [((held + pack, rank), F32)])
    (keep,) = call(own, operands, specs, [((held, rank), F32)], flops=10**9)

    chip_gram, own_sum, *outs = call(
        functools.partial(chip_kernel, piece),
        (keep, send, shifted(send, "col", 1, cols)),
        [VMEM] * 3,
        [((pack, rank), F32)] + [((piece, rank), F32)] * pairs,
    )
    grams = [chip_gram] + [shifted(chip_gram, "col", 2 * at, cols) for at in range(1, pairs)]
    pieces = [own_sum] + [shifted(out, "col", 2 * (at + 1), cols) for at, out in enumerate(outs)]
    (inverse,) = call(
        inverse_kernel, (time_gram, *grams), [VMEM] * (1 + pairs), [((rank, rank), F32)], flops=2 * 10**9
    )
    solved, squares = call(
        solve_kernel,
        (inverse, *pieces),
        [VMEM] * (1 + pairs),
        [((piece, rank), F32), ((rows * cols, rank), F32)],
    )
    squares = lax.all_to_all(squares, ("row", "col"), 0, 0, tiled=True)
    scales = jnp.sqrt(jnp.sum(squares, axis=0) / (own_rows * rows) + 1e-06)
    return solved / scales[None, :], scales


def solution(mesh):
    in_specs = (P(None, "row", "col"), P(("col", "row"), None), P())
    out_specs = (P(("row", "col"), None), P())
    return jax.shard_map(
        per_device, mesh=mesh, in_specs=in_specs, out_specs=out_specs, check_vma=False
    )
```

```python
import functools

import jax
import jax.numpy as jnp
from jax import lax
from jax.experimental import pallas as pl
from jax.experimental.pallas import tpu as pltpu
from jax.sharding import PartitionSpec as P

F32, BF16 = jnp.float32, jnp.bfloat16
HBM = pl.BlockSpec(memory_space=pltpu.HBM)
VMEM = pl.BlockSpec(memory_space=pltpu.VMEM)
TILE, STRIP, BLOCK = 8, 16, 32


def tdot(a, b):
    return lax.dot_general(a, b, (((0,), (0,)), ((), ())), preferred_element_type=F32)


def split3(x):
    hi = x.astype(BF16)
    rest = x - hi.astype(F32)
    mid = rest.astype(BF16)
    return hi, mid, (rest - mid.astype(F32)).astype(BF16)


def packed(square):
    size = square.shape[0]
    q, h = size // 4, size // 8
    return jnp.concatenate(
        [
            jnp.concatenate([square[2 * q : 3 * q, : 3 * q], square[:q, :q]], 1),
            square[3 * q :, :],
            jnp.concatenate([square[q : q + h, : 2 * q], square[q + h : 2 * q, : 2 * q]], 1),
        ],
        0,
    )


def unpacked(pack):
    size = pack.shape[1]
    q, h = size // 4, size // 8
    second = jnp.concatenate([pack[2 * q :, : 2 * q], pack[2 * q :, 2 * q :]], 0)
    lower = jnp.concatenate(
        [
            jnp.concatenate([pack[:q, 3 * q :], jnp.zeros((q, 3 * q), F32)], 1),
            jnp.concatenate([second, jnp.zeros((q, 2 * q), F32)], 1),
            jnp.concatenate([pack[:q, : 3 * q], jnp.zeros((q, q), F32)], 1),
            pack[q : 2 * q, :],
        ],
        0,
    )
    row = lax.broadcasted_iota(jnp.int32, (size, size), 0)
    col = lax.broadcasted_iota(jnp.int32, (size, size), 1)
    return jnp.where(col >= row, lower.T, lower)


def prepare_kernel(factor_ref, out_ref, own_ref):
    rows, rank = factor_ref.shape
    factor = factor_ref[...]
    low = factor.astype(BF16)
    residual = (factor - low.astype(F32)).astype(BF16)
    cross = tdot(low, residual)
    rest = packed((cross + cross.T + tdot(residual, residual)).astype(BF16))
    for ref in (out_ref, own_ref):
        ref[:rows, :] = low
        ref[rows:, :] = rest


def start_loads(owners, depth, tensor_ref, slots_ref, sems):
    row = lax.axis_index("row")
    arrivals = []
    for at, owner in enumerate(owners):
        start = 0
        if depth < tensor_ref.shape[2]:
            start = pl.multiple_of(lax.bitwise_xor(row, owner) * depth, depth)
        arrivals.append(
            pltpu.make_async_copy(
                tensor_ref.at[:, :, pl.ds(start, depth)], slots_ref.at[at], sems.at[at]
            )
        )
    for arrival in arrivals:
        arrival.start()
    return arrivals


def load_kernel(owners, depth, tensor_ref, time_ref, out_ref, gram_ref, slots_ref, sems):
    time_arrival = pltpu.make_async_copy(time_ref, out_ref, sems.at[len(owners)])
    time_arrival.start()
    arrivals = start_loads(owners, depth, tensor_ref, slots_ref, sems)
    time_arrival.wait()
    time = out_ref[...]
    gram_ref[...] = lax.dot_general(
        time,
        time,
        (((0,), (0,)), ((), ())),
        precision=lax.Precision.HIGHEST,
        preferred_element_type=F32,
    )
    for arrival in arrivals:
        arrival.wait()


def relay_kernel(ready_ref, part_ref, out_ref):
    del ready_ref
    out_ref[...] = part_ref[...]


def gram_of(parts, depth):
    gram, rest = 0.0, 0.0
    for part in parts:
        low = part[:depth, :]
        gram = gram + tdot(low, low)
        rest = rest + part[depth:, :].astype(F32)
    return packed(gram) + rest


def first_kernel(owners, depth, tensor_ref, time_ref, early_ref, *refs):
    parts, (result_ref, gram_ref, later_ref, sems) = refs[:-4], refs[-4:]
    arrivals = start_loads(owners, depth, tensor_ref, later_ref, sems)
    result_ref[...] = jnp.zeros(result_ref.shape, F32)

    @pl.loop(0, time_ref.shape[0])
    def _(snap):
        total = 0.0
        for at, part in enumerate(parts):
            total = total + jnp.dot(
                early_ref[at, snap], part[:depth, :], preferred_element_type=F32
            )
        result_ref[...] += total * time_ref[pl.ds(snap, 1), :]

    gram_ref[...] = gram_of(parts, depth)
    for arrival in arrivals:
        arrival.wait()


def last_kernel(depth, other, time_ref, early_ref, later_ref, result_ref, gram_ref, *refs):
    parts, out_ref = refs[:-1], refs[-1]
    col, cols = lax.axis_index("col"), lax.axis_size("col")
    piece = result_ref.shape[0] // cols
    side = lax.rem(col + other, 2)
    begin, later = early_ref.shape[0], later_ref.shape[0]
    blocks = [early_ref.at[at] for at in range(begin)]
    blocks = (blocks + [later_ref.at[at] for at in range(later)])[begin + later - len(parts) :]
    for pair in range(cols // 2):
        rows = pl.ds(pl.multiple_of((2 * pair + side) * piece, piece), piece)
        total = result_ref[rows, :]
        for snap in range(time_ref.shape[0] if parts else 0):
            product = sum(
                jnp.dot(block[snap, rows, :], part[:depth, :], preferred_element_type=F32)
                for block, part in zip(blocks, parts)
            )
            total = total + product * time_ref[snap : snap + 1, :]
        out_ref[pair * piece : (pair + 1) * piece, :] = total
    if other:
        gram = gram_ref[...]
        if parts:
            gram = gram + gram_of(parts, depth)
        out_ref[(cols // 2) * piece :, :] = gram


def chip_kernel(piece, keep_ref, sent_ref, got_ref, gram_ref, *out_refs):
    place = lax.div(lax.axis_index("col"), 2)
    held = keep_ref.shape[0]
    gram_ref[...] = sent_ref[held:, :] + got_ref[held:, :]
    for offset, out_ref in enumerate(out_refs):
        start = pl.multiple_of(lax.bitwise_xor(place, offset) * piece, piece)
        out_ref[...] = keep_ref[pl.ds(start, piece), :] + got_ref[pl.ds(start, piece), :]


def negative_inverse(matrix):
    size = matrix.shape[0]
    tiles = BLOCK // TILE
    lane = lax.broadcasted_iota(jnp.int32, (TILE, size), 1)
    sub = lax.broadcasted_iota(jnp.int32, (TILE, size), 0)
    at_row = lax.broadcasted_iota(jnp.int32, (size, size), 0)
    at_col = lax.broadcasted_iota(jnp.int32, (size, size), 1)

    def spread(value, row):
        return jnp.broadcast_to(value[row : row + 1, :], (TILE, size))

    for begin in range(0, size, BLOCK):
        end = begin + BLOCK
        work = [matrix[begin + TILE * t : begin + TILE * (t + 1), :] for t in range(tiles)]
        solved = [None] * tiles
        for strip in range(0, BLOCK, STRIP):
            cols = [
                {
                    t: jnp.broadcast_to(work[t][:, at : at + 1], (TILE, size))
                    for t in range(strip // TILE, tiles)
                }
                for at in range(begin + strip, begin + strip + STRIP)
            ]
            for k in range(STRIP):
                tile, row = divmod(strip + k, TILE)
                scale = lax.rsqrt(spread(cols[k][tile], row))
                here = lane == begin + strip + k
                pivot = jnp.where(here, -1.0, spread(work[tile], row)) * scale
                solved[tile] = pivot if row == 0 else jnp.where(sub >= row, pivot, solved[tile])
                lower = {t: cols[k][t] * scale for t in range(tile, tiles)}
                lower[tile] = jnp.where(sub > row, lower[tile], 0.0)
                for j in range(k + 1, STRIP):
                    its_tile, its_row = divmod(strip + j, TILE)
                    if its_tile == tile:
                        factor = spread(cols[j][tile], row) * scale
                    else:
                        factor = spread(lower[its_tile], its_row)
                    for t in range(its_tile, tiles):
                        cols[j][t] = cols[j][t] - lower[t] * factor
                for t in range(tile, tiles):
                    work[t] = jnp.where(here, 0.0, work[t]) - lower[t] * pivot
        row_of = lax.broadcasted_iota(jnp.int32, (BLOCK, size), 0) + begin
        col_of = lax.broadcasted_iota(jnp.int32, (BLOCK, size), 1)
        upper = (col_of > row_of) & (col_of < end)
        hi, mid, lo = split3(jnp.where(upper, 0.0, jnp.concatenate(solved, 0)))
        update = tdot(
            jnp.concatenate([hi, hi, mid, mid, hi, lo], 0),
            jnp.concatenate([hi, mid, hi, mid, lo, hi], 0),
        )
        swept = (at_row >= begin) & (at_row < end) | (at_col >= begin) & (at_col < end)
        matrix = jnp.where(swept, 0.0, matrix) - update
    return matrix


def inverse_kernel(time_gram_ref, *refs):
    grams, inverse_ref = refs[:-1], refs[-1]
    gram = unpacked(sum(ref[...] for ref in grams))
    inverse_ref[...] = negative_inverse(gram * time_gram_ref[...])


def solve_kernel(inverse_ref, *refs):
    sums, (solved_ref, squares_ref) = refs[:-2], refs[-2:]
    solved = -jnp.dot(
        sum(ref[...] for ref in sums),
        inverse_ref[...],
        precision=lax.Precision.HIGHEST,
        preferred_element_type=F32,
    )
    solved_ref[...] = solved
    squares = jnp.sum(solved * solved, axis=0, keepdims=True)
    squares_ref[...] = jnp.broadcast_to(squares, squares_ref.shape)


def shifted(value, axis, offset, groups):
    return lax.ppermute(value, axis, [(at, at ^ offset) for at in range(groups)])


def call(kernel, operands, in_specs, outs, scratch=(), room=24, flops=0):
    return pl.pallas_call(
        kernel,
        out_shape=tuple(jax.ShapeDtypeStruct(shape, dtype) for shape, dtype in outs),
        in_specs=in_specs,
        out_specs=(VMEM,) * len(outs),
        scratch_shapes=scratch,
        cost_estimate=pl.CostEstimate(flops=flops, bytes_accessed=0, transcendentals=0) if flops else None,
        compiler_params=pltpu.CompilerParams(vmem_limit_bytes=room * 2**20),
    )(*operands)


def per_device(tensor, second_factor, time_factor):
    snaps, own_rows, own_cols = tensor.shape
    depth, rank = second_factor.shape
    rows, cols = lax.axis_size("row"), lax.axis_size("col")
    piece = own_rows // cols
    pairs = cols // 2

    pack = rank * 5 // 8
    whole = ((depth + pack, rank), BF16)
    message, own = call(prepare_kernel, (second_factor,), [VMEM], [whole, whole])
    half = rows // 2
    near = sorted(range(1, half), key=lambda at: (bin(at).count("0") - len(bin(at)), at))
    opposite = shifted(message, "row", half, rows)
    arrived = {at: shifted(message, "row", at, rows) for at in near}
    in_hbm = pltpu.with_memory_space_constraint(tensor, pltpu.HBM)
    direct = depth % 128 == 0
    owners, width = ([0, *near, half, *(half + at for at in near)], depth) if direct else ([0], own_cols)
    block = (snaps, own_rows, width)
    begin, split = (half + 1, half + 1) if direct else (1, 1)
    time, time_gram, early = call(
        functools.partial(load_kernel, owners[:begin], width),
        (in_hbm, pltpu.with_memory_space_constraint(time_factor, pltpu.HBM)),
        [HBM, HBM],
        [((snaps, rank), F32), ((rank, rank), F32), ((begin, *block), BF16)],
        [pltpu.SemaphoreType.DMA((begin + 1,))],
    )
    (opposite,) = call(relay_kernel, (time, opposite), [VMEM] * 2, [whole])
    arrived[0], arrived[half] = own, opposite
    for at in near:
        arrived[half + at] = shifted(opposite, "row", at, rows)

    if direct:
        parts = [arrived[at] for at in owners]
    else:
        row = lax.axis_index("row")
        low = jnp.stack([arrived[at][:depth] for at in range(rows)])
        low = low[jnp.arange(rows) ^ row].reshape(rows * depth, rank)
        rest = sum(arrived[at][depth:].astype(F32) for at in range(rows)).astype(BF16)
        parts = [jnp.concatenate([low, rest], 0)]
    later = max(len(owners) - begin, 1)
    sums = [((own_rows, rank), F32), ((pack, rank), F32)]
    result, gram, tensor_later = call(
        functools.partial(first_kernel, owners[begin:], width),
        (in_hbm, time, early, *parts[:split]),
        [HBM] + [VMEM] * (2 + split),
        sums + [((later, *block), BF16)],
        [pltpu.SemaphoreType.DMA((later,))],
    )
    last = parts[split:]
    held = pairs * piece
    operands = (time, early, tensor_later, result, gram, *last)
    specs = [VMEM] * len(operands)
    other, own = functools.partial(last_kernel, width, 1), functools.partial(last_kernel, width, 0)
    (send,) = call(other, operands, specs, [((held + pack, rank), F32)])
    (keep,) = call(own, operands, specs, [((held, rank), F32)], flops=10**9)

    chip_gram, own_sum, *outs = call(
        functools.partial(chip_kernel, piece),
        (keep, send, shifted(send, "col", 1, cols)),
        [VMEM] * 3,
        [((pack, rank), F32)] + [((piece, rank), F32)] * pairs,
    )
    grams = [chip_gram] + [shifted(chip_gram, "col", 2 * at, cols) for at in range(1, pairs)]
    pieces = [own_sum] + [shifted(out, "col", 2 * (at + 1), cols) for at, out in enumerate(outs)]
    (inverse,) = call(
        inverse_kernel, (time_gram, *grams), [VMEM] * (1 + pairs), [((rank, rank), F32)], flops=2 * 10**9
    )
    solved, squares = call(
        solve_kernel,
        (inverse, *pieces),
        [VMEM] * (1 + pairs),
        [((piece, rank), F32), ((rows * cols, rank), F32)],
    )
    squares = lax.all_to_all(squares, ("row", "col"), 0, 0, tiled=True)
    scales = jnp.sqrt(jnp.sum(squares, axis=0) / (own_rows * rows) + 1e-06)
    return solved / scales[None, :], scales


def solution(mesh):
    in_specs = (P(None, "row", "col"), P(("col", "row"), None), P())
    out_specs = (P(("row", "col"), None), P())
    return jax.shard_map(
        per_device, mesh=mesh, in_specs=in_specs, out_specs=out_specs, check_vma=False
    )
```

```python
import functools

import jax
import jax.numpy as jnp
from jax import lax
from jax.experimental import pallas as pl
from jax.experimental.pallas import tpu as pltpu
from jax.sharding import PartitionSpec as P

F32, BF16 = jnp.float32, jnp.bfloat16
HBM = pl.BlockSpec(memory_space=pltpu.HBM)
VMEM = pl.BlockSpec(memory_space=pltpu.VMEM)
TILE, STRIP, BLOCK = 8, 16, 32


def tdot(a, b):
    return lax.dot_general(a, b, (((0,), (0,)), ((), ())), preferred_element_type=F32)


def split3(x):
    hi = x.astype(BF16)
    rest = x - hi.astype(F32)
    mid = rest.astype(BF16)
    return hi, mid, (rest - mid.astype(F32)).astype(BF16)


def packed(square):
    size = square.shape[0]
    q, h = size // 4, size // 8
    return jnp.concatenate(
        [
            jnp.concatenate([square[2 * q : 3 * q, : 3 * q], square[:q, :q]], 1),
            square[3 * q :, :],
            jnp.concatenate([square[q : q + h, : 2 * q], square[q + h : 2 * q, : 2 * q]], 1),
        ],
        0,
    )


def unpacked(pack):
    size = pack.shape[1]
    q, h = size // 4, size // 8
    second = jnp.concatenate([pack[2 * q :, : 2 * q], pack[2 * q :, 2 * q :]], 0)
    lower = jnp.concatenate(
        [
            jnp.concatenate([pack[:q, 3 * q :], jnp.zeros((q, 3 * q), F32)], 1),
            jnp.concatenate([second, jnp.zeros((q, 2 * q), F32)], 1),
            jnp.concatenate([pack[:q, : 3 * q], jnp.zeros((q, q), F32)], 1),
            pack[q : 2 * q, :],
        ],
        0,
    )
    row = lax.broadcasted_iota(jnp.int32, (size, size), 0)
    col = lax.broadcasted_iota(jnp.int32, (size, size), 1)
    return jnp.where(col >= row, lower.T, lower)


def prepare_kernel(factor_ref, out_ref, own_ref):
    rows, rank = factor_ref.shape
    factor = factor_ref[...]
    low = factor.astype(BF16)
    residual = (factor - low.astype(F32)).astype(BF16)
    cross = tdot(low, residual)
    rest = packed((cross + cross.T + tdot(residual, residual)).astype(BF16))
    for ref in (out_ref, own_ref):
        ref[:rows, :] = low
        ref[rows:, :] = rest


def start_loads(owners, depth, tensor_ref, slots_ref, sems):
    row = lax.axis_index("row")
    arrivals = []
    for at, owner in enumerate(owners):
        start = 0
        if depth < tensor_ref.shape[2]:
            start = pl.multiple_of(lax.bitwise_xor(row, owner) * depth, depth)
        arrivals.append(
            pltpu.make_async_copy(
                tensor_ref.at[:, :, pl.ds(start, depth)], slots_ref.at[at], sems.at[at]
            )
        )
    for arrival in arrivals:
        arrival.start()
    return arrivals


def load_kernel(owners, depth, tensor_ref, time_ref, out_ref, gram_ref, slots_ref, sems):
    time_arrival = pltpu.make_async_copy(time_ref, out_ref, sems.at[len(owners)])
    time_arrival.start()
    arrivals = start_loads(owners, depth, tensor_ref, slots_ref, sems)
    time_arrival.wait()
    time = out_ref[...]
    gram_ref[...] = lax.dot_general(
        time,
        time,
        (((0,), (0,)), ((), ())),
        precision=lax.Precision.HIGHEST,
        preferred_element_type=F32,
    )
    for arrival in arrivals:
        arrival.wait()


def relay_kernel(ready_ref, part_ref, out_ref):
    del ready_ref
    out_ref[...] = part_ref[...]


def gram_of(parts, depth):
    gram, rest = 0.0, 0.0
    for part in parts:
        low = part[:depth, :]
        gram = gram + tdot(low, low)
        rest = rest + part[depth:, :].astype(F32)
    return packed(gram) + rest


def first_kernel(owners, depth, tensor_ref, time_ref, early_ref, *refs):
    parts, (result_ref, gram_ref, later_ref, sems) = refs[:-4], refs[-4:]
    arrivals = start_loads(owners, depth, tensor_ref, later_ref, sems)
    result_ref[...] = jnp.zeros(result_ref.shape, F32)

    @pl.loop(0, time_ref.shape[0])
    def _(snap):
        total = 0.0
        for at, part in enumerate(parts):
            total = total + jnp.dot(
                early_ref[at, snap], part[:depth, :], preferred_element_type=F32
            )
        result_ref[...] += total * time_ref[pl.ds(snap, 1), :]

    gram_ref[...] = gram_of(parts, depth)
    for arrival in arrivals:
        arrival.wait()


def last_kernel(depth, other, time_ref, early_ref, later_ref, result_ref, gram_ref, *refs):
    parts, out_ref = refs[:-1], refs[-1]
    col, cols = lax.axis_index("col"), lax.axis_size("col")
    piece = result_ref.shape[0] // cols
    side = lax.rem(col + other, 2)
    begin, later = early_ref.shape[0], later_ref.shape[0]
    blocks = [early_ref.at[at] for at in range(begin)]
    blocks = (blocks + [later_ref.at[at] for at in range(later)])[begin + later - len(parts) :]
    for pair in range(cols // 2):
        rows = pl.ds(pl.multiple_of((2 * pair + side) * piece, piece), piece)
        total = result_ref[rows, :]
        for snap in range(time_ref.shape[0] if parts else 0):
            product = sum(
                jnp.dot(block[snap, rows, :], part[:depth, :], preferred_element_type=F32)
                for block, part in zip(blocks, parts)
            )
            total = total + product * time_ref[snap : snap + 1, :]
        out_ref[pair * piece : (pair + 1) * piece, :] = total
    if other:
        gram = gram_ref[...]
        if parts:
            gram = gram + gram_of(parts, depth)
        out_ref[(cols // 2) * piece :, :] = gram


def chip_kernel(piece, keep_ref, sent_ref, got_ref, gram_ref, *out_refs):
    place = lax.div(lax.axis_index("col"), 2)
    held = keep_ref.shape[0]
    gram_ref[...] = sent_ref[held:, :] + got_ref[held:, :]
    for offset, out_ref in enumerate(out_refs):
        start = pl.multiple_of(lax.bitwise_xor(place, offset) * piece, piece)
        out_ref[...] = keep_ref[pl.ds(start, piece), :] + got_ref[pl.ds(start, piece), :]


def negative_inverse(matrix):
    size = matrix.shape[0]
    tiles = BLOCK // TILE
    lane = lax.broadcasted_iota(jnp.int32, (TILE, size), 1)
    sub = lax.broadcasted_iota(jnp.int32, (TILE, size), 0)
    at_row = lax.broadcasted_iota(jnp.int32, (size, size), 0)
    at_col = lax.broadcasted_iota(jnp.int32, (size, size), 1)

    def spread(value, row):
        return jnp.broadcast_to(value[row : row + 1, :], (TILE, size))

    for begin in range(0, size, BLOCK):
        end = begin + BLOCK
        work = [matrix[begin + TILE * t : begin + TILE * (t + 1), :] for t in range(tiles)]
        solved = [None] * tiles
        for strip in range(0, BLOCK, STRIP):
            cols = [
                {
                    t: jnp.broadcast_to(work[t][:, at : at + 1], (TILE, size))
                    for t in range(strip // TILE, tiles)
                }
                for at in range(begin + strip, begin + strip + STRIP)
            ]
            for k in range(STRIP):
                tile, row = divmod(strip + k, TILE)
                scale = lax.rsqrt(spread(cols[k][tile], row))
                here = lane == begin + strip + k
                pivot = jnp.where(here, -1.0, spread(work[tile], row)) * scale
                solved[tile] = pivot if row == 0 else jnp.where(sub >= row, pivot, solved[tile])
                lower = {t: cols[k][t] * scale for t in range(tile, tiles)}
                lower[tile] = jnp.where(sub > row, lower[tile], 0.0)
                for j in range(k + 1, STRIP):
                    its_tile, its_row = divmod(strip + j, TILE)
                    if its_tile == tile:
                        factor = spread(cols[j][tile], row) * scale
                    else:
                        factor = spread(lower[its_tile], its_row)
                    for t in range(its_tile, tiles):
                        cols[j][t] = cols[j][t] - lower[t] * factor
                for t in range(tile, tiles):
                    work[t] = jnp.where(here, 0.0, work[t]) - lower[t] * pivot
        row_of = lax.broadcasted_iota(jnp.int32, (BLOCK, size), 0) + begin
        col_of = lax.broadcasted_iota(jnp.int32, (BLOCK, size), 1)
        upper = (col_of > row_of) & (col_of < end)
        hi, mid, lo = split3(jnp.where(upper, 0.0, jnp.concatenate(solved, 0)))
        update = tdot(
            jnp.concatenate([hi, hi, mid, mid, hi, lo], 0),
            jnp.concatenate([hi, mid, hi, mid, lo, hi], 0),
        )
        swept = (at_row >= begin) & (at_row < end) | (at_col >= begin) & (at_col < end)
        matrix = jnp.where(swept, 0.0, matrix) - update
    return matrix


def inverse_kernel(time_gram_ref, *refs):
    grams, inverse_ref = refs[:-1], refs[-1]
    gram = unpacked(sum(ref[...] for ref in grams))
    inverse_ref[...] = negative_inverse(gram * time_gram_ref[...])


def solve_kernel(inverse_ref, *refs):
    sums, (solved_ref, squares_ref) = refs[:-2], refs[-2:]
    solved = -jnp.dot(
        sum(ref[...] for ref in sums),
        inverse_ref[...],
        precision=lax.Precision.HIGHEST,
        preferred_element_type=F32,
    )
    solved_ref[...] = solved
    squares = jnp.sum(solved * solved, axis=0, keepdims=True)
    squares_ref[...] = jnp.broadcast_to(squares, squares_ref.shape)


def shifted(value, axis, offset, groups):
    return lax.ppermute(value, axis, [(at, at ^ offset) for at in range(groups)])


def call(kernel, operands, in_specs, outs, scratch=(), room=24, flops=0):
    return pl.pallas_call(
        kernel,
        out_shape=tuple(jax.ShapeDtypeStruct(shape, dtype) for shape, dtype in outs),
        in_specs=in_specs,
        out_specs=(VMEM,) * len(outs),
        scratch_shapes=scratch,
        cost_estimate=pl.CostEstimate(flops=flops, bytes_accessed=0, transcendentals=0) if flops else None,
        compiler_params=pltpu.CompilerParams(vmem_limit_bytes=room * 2**20),
    )(*operands)


def per_device(tensor, second_factor, time_factor):
    snaps, own_rows, own_cols = tensor.shape
    depth, rank = second_factor.shape
    rows, cols = lax.axis_size("row"), lax.axis_size("col")
    piece = own_rows // cols
    pairs = cols // 2

    pack = rank * 5 // 8
    whole = ((depth + pack, rank), BF16)
    message, own = call(prepare_kernel, (second_factor,), [VMEM], [whole, whole])
    half = rows // 2
    near = sorted(range(1, half), key=lambda at: (bin(at).count("0") - len(bin(at)), at))
    opposite = shifted(message, "row", half, rows)
    arrived = {at: shifted(message, "row", at, rows) for at in near}
    in_hbm = pltpu.with_memory_space_constraint(tensor, pltpu.HBM)
    direct = depth % 128 == 0
    owners, width = ([0, *range(1, half), half, *(half + at for at in near)], depth) if direct else ([0], own_cols)
    block = (snaps, own_rows, width)
    begin, split = (half + 1, half + 1) if direct else (1, 1)
    time, time_gram, early = call(
        functools.partial(load_kernel, owners[:begin], width),
        (in_hbm, pltpu.with_memory_space_constraint(time_factor, pltpu.HBM)),
        [HBM, HBM],
        [((snaps, rank), F32), ((rank, rank), F32), ((begin, *block), BF16)],
        [pltpu.SemaphoreType.DMA((begin + 1,))],
    )
    (opposite,) = call(relay_kernel, (time, opposite), [VMEM] * 2, [whole])
    arrived[0], arrived[half] = own, opposite
    for at in near:
        arrived[half + at] = shifted(opposite, "row", at, rows)

    if direct:
        parts = [arrived[at] for at in owners]
    else:
        row = lax.axis_index("row")
        low = jnp.stack([arrived[at][:depth] for at in range(rows)])
        low = low[jnp.arange(rows) ^ row].reshape(rows * depth, rank)
        rest = sum(arrived[at][depth:].astype(F32) for at in range(rows)).astype(BF16)
        parts = [jnp.concatenate([low, rest], 0)]
    later = max(len(owners) - begin, 1)
    sums = [((own_rows, rank), F32), ((pack, rank), F32)]
    result, gram, tensor_later = call(
        functools.partial(first_kernel, owners[begin:], width),
        (in_hbm, time, early, *parts[:split]),
        [HBM] + [VMEM] * (2 + split),
        sums + [((later, *block), BF16)],
        [pltpu.SemaphoreType.DMA((later,))],
    )
    last = parts[split:]
    held = pairs * piece
    operands = (time, early, tensor_later, result, gram, *last)
    specs = [VMEM] * len(operands)
    other, own = functools.partial(last_kernel, width, 1), functools.partial(last_kernel, width, 0)
    (send,) = call(other, operands, specs, [((held + pack, rank), F32)])
    (keep,) = call(own, operands, specs, [((held, rank), F32)], flops=10**9)

    chip_gram, own_sum, *outs = call(
        functools.partial(chip_kernel, piece),
        (keep, send, shifted(send, "col", 1, cols)),
        [VMEM] * 3,
        [((pack, rank), F32)] + [((piece, rank), F32)] * pairs,
    )
    grams = [chip_gram] + [shifted(chip_gram, "col", 2 * at, cols) for at in range(1, pairs)]
    pieces = [own_sum] + [shifted(out, "col", 2 * (at + 1), cols) for at, out in enumerate(outs)]
    (inverse,) = call(
        inverse_kernel, (time_gram, *grams), [VMEM] * (1 + pairs), [((rank, rank), F32)], flops=2 * 10**9
    )
    solved, squares = call(
        solve_kernel,
        (inverse, *pieces),
        [VMEM] * (1 + pairs),
        [((piece, rank), F32), ((rows * cols, rank), F32)],
    )
    squares = lax.all_to_all(squares, ("row", "col"), 0, 0, tiled=True)
    scales = jnp.sqrt(jnp.sum(squares, axis=0) / (own_rows * rows) + 1e-06)
    return solved / scales[None, :], scales


def solution(mesh):
    in_specs = (P(None, "row", "col"), P(("col", "row"), None), P())
    out_specs = (P(("row", "col"), None), P())
    return jax.shard_map(
        per_device, mesh=mesh, in_specs=in_specs, out_specs=out_specs, check_vma=False
    )
```
